128 devices in a mesh: pts: 32 (over z_hi, x, y), lm: 4 (over z_lo, core).
Axes of the slice: x: 4, y: 4, z: 4 (z_hi: 2, z_lo: 2; z = z_hi * 2 + z_lo), core: 2. Of those that a mesh axis runs over, the one named last changes fastest.
Arguments:
- kernel_features: float32 [32768, 2048], P('pts', 'lm'), may hold values from -6 to 6
- factor: float32 [2048, 2048], P(None, 'lm'), may hold values from -0.125 to 0.125
- diag_inverse: float32 [4, 512, 512], P('lm'), as said below
- block_order: int32 [16], replicated, may hold values from 0 to 15, each once
Outputs:
- gram: float32 [2048, 2048], P('pts', 'lm')
The draws below stay inside these ranges and needn't reach their ends.
Inputs may be any that keep to these rules, and one draw needn't show every extreme that they name: `block_order`: a permutation of the 16 cluster blocks. `diag_inverse`: each block is upper triangular.
All inputs are finite; a program needn't handle non-finite values.
Results may differ from the reference program's by a relative error of at most 0.0001.
Values sent between devices are 32-bit elements; how exact they have to be, the bound alone decides.
No kernel may reach another device: no remote copies, remote signals or barrier semaphores. Data moves between devices by JAX's collectives and lax.ppermute only.
A program may use at most 128 MiB of HBM per device.

```python
import jax
import jax.numpy as jnp
from jax import lax

PANEL = 512
CLUSTER = 128
PANELS = 4
LANDMARKS = 2048
NBLK = 16
POINTS = 32768
N_LM = 4


def draw_diag_inverse(key, part):
    key = jax.random.fold_in(key, 7)
    first, second = jax.random.split(key)
    diagonal = jax.random.uniform(first, (PANELS, PANEL), jnp.float32, 0.5, 2.0)
    spread = jax.random.normal(second, (PANELS, PANEL, PANEL), jnp.float32) * (0.4 / PANEL ** 0.5)
    rowsi = jnp.arange(PANEL)[:, None]
    colsi = jnp.arange(PANEL)[None, :]
    strict = (colsi > rowsi).astype(jnp.float32)
    ident = (colsi == rowsi).astype(jnp.float32)
    return spread * strict[None] + diagonal[:, :, None] * ident[None]


def block_levels(stream_key, extent, pieces, least, high):
    def one(axis_at, parts):
        steps = jax.random.uniform(jax.random.fold_in(jax.random.fold_in(stream_key, 6), axis_at), (parts,), jnp.float32, least / len(pieces), high / len(pieces))
        return jnp.repeat(jnp.exp(steps), extent[axis_at] // parts).reshape((-1,) + (1,) * (len(extent) - axis_at - 1))

    level = one(*pieces[0])
    for cut in pieces[1:]:
        level = level * one(*cut)
    return level


def noise(rng, extent, width, bound, pieces=(), kind=jnp.bfloat16):
    level = block_levels(rng, extent, pieces, -0.22, 0.18) if pieces else 1.0
    entries = jax.random.normal(rng, extent, jnp.float32) * width * level
    return jnp.minimum(jnp.maximum(entries, -bound), bound).astype(kind)


def setup_inputs(seed: int = 0) -> dict:
    key_of = jax.random.split(jax.random.key(seed), 5)
    kernel_features = noise(key_of[0], (POINTS, LANDMARKS), 1.0, 6.0, ((0, 32), (1, 4)), jnp.float32)
    factor = noise(key_of[1], (LANDMARKS, LANDMARKS), (PANEL * N_LM) ** -0.5, 0.125, ((1, 4),), jnp.float32)
    diag_inverse = draw_diag_inverse(jax.random.fold_in(key_of[4], 71), 0)
    block_order = jax.random.permutation(key_of[3], NBLK).astype(jnp.int32)
    return dict(kernel_features=kernel_features, factor=factor, diag_inverse=diag_inverse, block_order=block_order)


def reference(kernel_features, factor, diag_inverse, block_order):
    precise = lax.Precision.HIGHEST
    columns = (block_order[:, None] * CLUSTER + jnp.arange(CLUSTER, dtype=jnp.int32)[None, :]).reshape(-1).astype(jnp.int32)
    ordered = jnp.take(kernel_features, columns, axis=1)
    solved = []
    for panel_id in range(PANELS):
        running = ordered[:, panel_id * PANEL:(panel_id + 1) * PANEL]
        for earlier in range(panel_id):
            block = factor[earlier * PANEL:(earlier + 1) * PANEL, panel_id * PANEL:(panel_id + 1) * PANEL]
            running = running - jnp.dot(solved[earlier], block, precision=precise)
        solved.append(jnp.dot(running, diag_inverse[panel_id], precision=precise))
    total = LANDMARKS
    outcols = []
    for panel_id in range(PANELS):
        upper = jnp.concatenate(solved[:panel_id + 1], axis=1)
        part = lax.dot_general(upper, solved[panel_id], (((0,), (0,)), ((), ())), precision=precise) / float(POINTS)
        below = jnp.zeros((total - (panel_id + 1) * PANEL, PANEL), jnp.float32)
        outcols.append(jnp.concatenate([part, below], axis=0))
    return jnp.concatenate(outcols, axis=1)
```

```python
import jax
import jax.numpy as jnp
from jax import lax
from jax.sharding import PartitionSpec as P

PANEL = 512
CLUSTER = 128
ROWS = 64
HIGH = lax.Precision.HIGH

CELLS = [(zh, x, y) for zh in range(2) for x in range(4) for y in range(4)]


def pts_index(zh, x, y):
    return (zh * 4 + x) * 4 + y


def along_x(step):
    return [(pts_index(z, x, y), pts_index(z, (x + step) % 4, y)) for z, x, y in CELLS]


def along_y(step):
    return [(pts_index(z, x, y), pts_index(z, x, (y + step) % 4)) for z, x, y in CELLS]


OTHER_HIGH = [(pts_index(z, x, y), pts_index(1 - z, x, y)) for z, x, y in CELLS]
OTHER_CHIP = [(k, k ^ 2) for k in range(4)]
OTHER_CORE = [(k, k ^ 1) for k in range(4)]


def flip(k):
    return [
        ((8 * a + b) * 4 + j, (8 * j + (b ^ k)) * 4 + a)
        for a in range(4)
        for b in range(8)
        for j in range(4)
    ]


def mm(a, b):
    return jnp.dot(a, b, precision=HIGH)


def tmm(a, b):
    return lax.dot_general(a, b, (((0,), (0,)), ((), ())), precision=HIGH)


def index_of(stack, k):
    return lax.dynamic_index_in_dim(stack, k, 0, keepdims=False)


def scatter_plane(first, second, x, y):
    a, b = index_of(first, x), lax.dynamic_index_in_dim(second, y, 1, keepdims=False)
    for step in (1, 3, 2):
        a += lax.ppermute(index_of(first, (x + step) % 4), "pts", along_x(step))
        b += lax.ppermute(
            lax.dynamic_index_in_dim(second, (y + step) % 4, 1, keepdims=False), "pts", along_y(step)
        )
    c, d = index_of(a, y), index_of(b, x)
    for step in (1, 3, 2):
        c += lax.ppermute(index_of(a, (y + step) % 4), "pts", along_y(step))
        d += lax.ppermute(index_of(b, (x + step) % 4), "pts", along_x(step))
    return c, d


def per_device(kernel_features, factor, diag_inverse, block_order):
    own = kernel_features
    points, panel = own.shape
    half = points // 2
    total = points * lax.axis_size("pts")
    i, j = lax.axis_index("pts"), lax.axis_index("lm")
    chip, core = j // 2, j % 2
    high, x, y = i // 16, (i // 4) % 4, i % 4
    group, member = i // 8, i % 8
    first_core, first_chip = core == 0, chip == 0

    sent = lax.dynamic_slice_in_dim(own, (1 - chip) * half, half)
    across = lax.ppermute(sent, "lm", OTHER_CHIP)
    pair = lax.ppermute(own, "lm", OTHER_CORE)

    inverse = diag_inverse[0]
    pair_inverse = lax.ppermute(inverse, "lm", OTHER_CORE)
    above = factor[: 2 * panel]
    pair_above = lax.ppermute(above, "lm", OTHER_CORE)
    link = lax.dynamic_slice_in_dim(factor, chip * 2 * panel, panel)
    corner = -mm(pair_inverse, mm(link, inverse))
    local = jnp.where(
        first_core,
        jnp.concatenate([inverse, jnp.zeros_like(inverse)], 0),
        jnp.concatenate([corner, inverse], 0),
    )
    far = mm(above, inverse) + jnp.where(first_core, 0.0, mm(pair_above, corner))

    diagonal = tmm(own, own) * 0.5
    beside = tmm(
        jnp.where(first_core, own, pair),
        jnp.where(first_core, pair[:, : panel // 2], own[:, panel // 2 :]),
    )
    own_half = lax.dynamic_slice_in_dim(own, chip * half, half)
    pair_half = lax.dynamic_slice_in_dim(pair, chip * half, half)
    cross_own = tmm(jnp.where(first_chip, own_half, across), jnp.where(first_chip, across, own_half))
    cross_pair = tmm(
        jnp.where(first_chip, pair_half, across), jnp.where(first_chip, across, pair_half)
    )

    def plane(a):
        return a.reshape(4, 4, panel // 16, a.shape[1])

    diagonal, beside, cross_own, cross_pair = map(plane, (diagonal, beside, cross_own, cross_pair))
    cut = 384
    d1, d2 = scatter_plane(
        diagonal[..., :cut], jnp.concatenate([diagonal[..., cut:], beside], -1), x, y
    )
    c1, c2 = scatter_plane(cross_own, cross_pair, x, y)
    mine = jnp.concatenate([d1, d2, c1, c2], -1)
    part = panel // 32
    mine = lax.dynamic_slice_in_dim(mine, high * part, part) + lax.ppermute(
        lax.dynamic_slice_in_dim(mine, (1 - high) * part, part), "pts", OTHER_HIGH
    )

    def spread(value):
        far_value = lax.ppermute(value, "lm", OTHER_CHIP)
        both = jnp.stack([value, far_value])
        other = lax.ppermute(both, "lm", OTHER_CORE)
        stack = jnp.stack([both[0], other[0], both[1], other[1]])
        return [index_of(stack, q ^ j) for q in range(4)]

    s0, s1, s2, s3 = spread(mine)
    wide, thin = panel, panel // 2

    def pick(s, at):
        edges = (0, wide, wide + thin, 2 * wide + thin, 3 * wide + thin)
        return s[:, edges[at] : edges[at + 1]]

    nothing = jnp.zeros((part, panel), jnp.float32)
    upper = jnp.concatenate(
        [
            jnp.concatenate(
                [
                    pick(s0, 0),
                    pick(s0, 1),
                    pick(s1, 1),
                    pick(s0, 2) + pick(s2, 2),
                    pick(s1, 3) + pick(s2, 3),
                ],
                1,
            ),
            jnp.concatenate(
                [nothing, pick(s1, 0), pick(s0, 3) + pick(s3, 3), pick(s1, 2) + pick(s3, 2)], 1
            ),
            jnp.concatenate([nothing, nothing, pick(s2, 0), pick(s2, 1), pick(s3, 1)], 1),
            jnp.concatenate([nothing, nothing, nothing, pick(s3, 0)], 1),
        ],
        0,
    )
    ordered = jnp.take(upper.reshape(ROWS, 16, CLUSTER), block_order, axis=1).reshape(ROWS, -1)

    def finish(near):
        got = lax.ppermute(near, "lm", OTHER_CHIP)
        got_pair = lax.ppermute(got, "lm", OTHER_CORE)
        before = jnp.where(
            first_core,
            jnp.concatenate([got, got_pair], 1),
            jnp.concatenate([got_pair, got], 1),
        )
        return near - jnp.where(first_chip, 0.0, mm(before, far))

    solved = finish(mm(lax.dynamic_slice_in_dim(ordered, chip * 2 * panel, 2 * panel, 1), local))

    def flipped(rows):
        blocks = rows.reshape(ROWS, 8, ROWS).transpose(1, 0, 2)
        got = jnp.stack(
            [lax.ppermute(index_of(blocks, member ^ k), ("pts", "lm"), flip(k)) for k in range(8)]
        )
        return jnp.take(got, jnp.arange(8) ^ member, axis=0)

    columns = jnp.concatenate(spread(flipped(solved)), 0)
    columns = columns.reshape(2, 16, 4, part, ROWS).transpose(2, 1, 0, 3, 4).reshape(16, CLUSTER, ROWS)
    columns = jnp.take(columns, block_order, axis=0).reshape(-1, ROWS)
    result = finish(tmm(lax.dynamic_slice_in_dim(columns, chip * 2 * panel, 2 * panel, 0), local))
    turned = flipped(result).transpose(2, 0, 1).reshape(ROWS, panel)
    return jnp.where(group <= j, (result + turned) / total, 0.0)


def solution(mesh):
    placed = (P("pts", "lm"), P(None, "lm"), P("lm", None, None), P())
    return jax.shard_map(
        per_device, mesh=mesh, in_specs=placed, out_specs=P("pts", "lm"), check_vma=False
    )
```

```python
import jax
import jax.numpy as jnp
from jax import lax
from jax.experimental import pallas as pl
from jax.experimental.pallas import tpu as pltpu
from jax.sharding import PartitionSpec as P

PANEL = 512
CLUSTER = 128
COSTS = (40, 6, 4, 4)
PIECES = ((0, 128), (128, 384))
ROWS = 64

CELLS = [(zh, x, y) for zh in range(2) for x in range(4) for y in range(4)]


def pts_index(zh, x, y):
    return (zh * 4 + x) * 4 + y


def plane_step(step, swapped):
    pairs = []
    for z, x, y in CELLS:
        for j in range(4):
            if (j % 2 == 0) != swapped:
                to = pts_index(z, (x + step) % 4, y)
            else:
                to = pts_index(z, x, (y + step) % 4)
            pairs.append((pts_index(z, x, y) * 4 + j, to * 4 + j))
    return pairs


def other_high(k):
    return [
        (pts_index(z, x, y) * 4 + j, pts_index(1 - z, x, y) * 4 + (j ^ k))
        for z, x, y in CELLS
        for j in range(4)
    ]


OTHER_CHIP = [(k, k ^ 2) for k in range(4)]
OTHER_CORE = [(k, k ^ 1) for k in range(4)]


def swap(k):
    return [
        ((8 * a + b) * 4 + j, (8 * j + b) * 4 + (a ^ k))
        for a in range(4)
        for b in range(8)
        for j in range(4)
    ]


EIGHTS = [[8 * a + b for b in range(8)] for a in range(4)]


def halves(value):
    first = value.astype(jnp.bfloat16)
    return first, (value - first.astype(jnp.float32)).astype(jnp.bfloat16)


def contract(a, b):
    def one(u, v):
        return lax.dot_general(u, v, (((0,), (0,)), ((), ())), preferred_element_type=jnp.float32)

    return one(a[0], b[0]) + (one(a[0], b[1]) + one(a[1], b[0]))


def multiply(a, b):
    def one(u, v):
        return jnp.dot(u, v, preferred_element_type=jnp.float32)

    return one(a[0], b[0]) + (one(a[0], b[1]) + one(a[1], b[0]))


def write_strips(place, product, outs):
    core, first, second = place[0], place[2], place[3]
    for k in range(4):
        for m in range(4):
            f, g = (first + k) % 4, (second + m) % 4
            strip = jnp.where(core == 0, 4 * f + g, 4 * g + f)
            outs[k][m] = product[pl.ds(pl.multiple_of(strip * 32, 32), 32), :]


def near_kernel(place, own, pair, product):
    panel = own.shape[1]
    thin = panel // 2
    a = halves(own[...])
    product[:, :panel] = contract(a, a) * 0.5

    @pl.when(place[0] == 0)
    def _():
        product[:, panel:] = contract(a, halves(pair[:, :thin]))

    @pl.when(place[0] != 0)
    def _():
        b = [part[:, thin:] for part in a]
        product[:, panel:] = contract(halves(pair[...]), b)


def across_kernel(place, own, pair, value, *refs):
    *others, out0, out1, out2, out3, product = refs
    half, width = value.shape
    rows = pl.ds(pl.multiple_of(place[1] * half, half), half)
    b = halves(value[...])
    start = product.shape[1] - 2 * width
    for other in others:
        product[:, :start] = other[...]
    product[:, start : start + width] = contract(halves(own[rows, :]), b)
    product[:, start + width :] = contract(halves(pair[rows, :]), b)
    write_strips(place, product, (out0, out1, out2, out3))


def inverse_kernel(
    place, inverse, pair_inverse, factor, pair_factor, near, near_low, far, far_low, above, pair_above, link, done
):
    panel = inverse.shape[0]
    start = pl.multiple_of(place[1] * 2 * panel, 2 * panel)
    copies = [
        pltpu.make_async_copy(factor.at[pl.ds(0, 2 * panel), :], above, done.at[0]),
        pltpu.make_async_copy(pair_factor.at[pl.ds(0, 2 * panel), :], pair_above, done.at[1]),
        pltpu.make_async_copy(factor.at[pl.ds(start, panel), :], link, done.at[2]),
    ]
    for copy in copies:
        copy.start()
    for copy in copies:
        copy.wait()
    d = halves(inverse[...])

    def put(high, low, rows, value):
        parts = halves(value)
        high[rows, :] = parts[0]
        low[rows, :] = parts[1]

    top, bottom = slice(0, panel), slice(panel, 2 * panel)

    @pl.when(place[0] == 0)
    def _():
        near[top, :], near_low[top, :] = d
        near[bottom, :] = jnp.zeros_like(d[0])
        near_low[bottom, :] = jnp.zeros_like(d[0])
        for rows in (top, bottom):
            put(far, far_low, rows, multiply(halves(above[rows, :]), d))

    @pl.when(place[0] != 0)
    def _():
        near[bottom, :], near_low[bottom, :] = d
        corner = -multiply(halves(pair_inverse[...]), halves(multiply(halves(link[...]), d)))
        put(near, near_low, top, corner)
        c = halves(corner)
        for rows in (top, bottom):
            value = multiply(halves(above[rows, :]), d) + multiply(halves(pair_above[rows, :]), c)
            put(far, far_low, rows, value)


def collect(place, held, value, far, other):
    j = place[4]
    held[j] = value[...]
    held[j ^ 2] = far[...]
    held[j ^ 1] = other[0]
    held[j ^ 3] = other[1]


def first_kernel(place, order, value, far, other, near, near_low, out, held, upper, ordered):
    part = value.shape[0]
    panel = near.shape[1]
    thin = panel // 2
    collect(place, held, value, far, other)

    def put(q, column, source, first, width):
        upper[part * q : part * (q + 1), column : column + width] = held[
            source, :, first : first + width
        ]

    for q in range(4):
        chip, core = divmod(q, 2)
        put(q, q * panel, q, 0, panel)
        if core == 0:
            put(q, (q + 1) * panel, q, panel, thin)
            put(q, (q + 1) * panel + thin, q + 1, panel, thin)
        else:
            upper[part * q : part * (q + 1), (q - 1) * panel : q * panel] = jnp.zeros(
                (part, panel), jnp.float32
            )
        for c in range(2):
            first = panel + thin
            for at, width in PIECES:
                column = (2 * (1 - chip) + c) * panel + at
                put(q, column, q if c == core else q ^ 1, first + width * (c != core), width)
                first += 2 * width
    for k in range(8):
        block = order[place[1] * 8 + k]
        ordered[:, k * CLUSTER : (k + 1) * CLUSTER] = upper[
            :, pl.ds(pl.multiple_of(block * CLUSTER, CLUSTER), CLUSTER)
        ]
    out[...] = multiply(halves(ordered[...]), (near[...], near_low[...]))


def less_far(place, value, got, got_pair, far, far_low, solved):
    panel = value.shape[1]
    solved[...] = value[...]

    @pl.when(place[1] != 0)
    def _():
        core = place[0]
        rows = [pl.ds(pl.multiple_of(c * panel, panel), panel) for c in (core, 1 - core)]
        total = value[...]
        for source, r in zip((got, got_pair), rows):
            total -= multiply(halves(source[...]), (far[r, :], far_low[r, :]))
        solved[...] = total


def pack(solved, out):
    left = lax.broadcasted_iota(jnp.int32, (32, 2 * ROWS), 1) < ROWS
    for g in range(4):
        low = solved[:32, g * 2 * ROWS : (g + 1) * 2 * ROWS]
        high = solved[32:, g * 2 * ROWS : (g + 1) * 2 * ROWS]
        out[2 * g] = jnp.where(left, low, pltpu.roll(high, ROWS, 1))
        out[2 * g + 1] = jnp.where(left, pltpu.roll(low, ROWS, 1), high)


def second_kernel(place, value, got, got_pair, far, far_low, solved, out):
    less_far(place, value, got, got_pair, far, far_low, solved)
    pack(solved, out)


def third_kernel(place, order, value, far, other, near, near_low, out, held, rows, ordered):
    part = value.shape[1] // 2
    collect(place, held, value, far, other)
    for a in range(4):
        for b in range(8):
            high, strip = a // 2, 8 * (a % 2) + b
            for q in range(2):
                start = 512 * q + 32 * strip + part * high
                rows[start : start + part, :] = held[a, b, part * q : part * (q + 1), :]
    for k in range(8):
        block = order[place[1] * 8 + k]
        taken = rows[pl.ds(pl.multiple_of((block % 8) * CLUSTER, CLUSTER), CLUSTER), :]
        ordered[k * CLUSTER : (k + 1) * CLUSTER, :] = jnp.where(
            block >= 8, pltpu.roll(taken, ROWS, 1), taken
        )
    out[...] = contract(halves(ordered[...]), (near[...], near_low[...]))[:ROWS]


def last_kernel(place, scale, result, turned, out, rows):
    for b in range(8):
        rows[64 * b : 64 * b + 32, :] = turned[b]
        rows[64 * b + 32 : 64 * b + 64, :] = pltpu.roll(turned[b], ROWS, 1)
    both = (result[...] + rows[...].T[:ROWS]) * scale[0]
    out[...] = jnp.where(place[5] <= place[4], both, 0.0)


def kernel_call(kernel, scalars, out_shape, scratch, cost, *arrays, after=(), large=(), large_outs=0):
    arrays = (*arrays, *large)
    inputs = len(scalars) + len(arrays)

    def body(*refs):
        kernel(*refs[:inputs], *refs[inputs + len(after) :])

    vmem = pl.BlockSpec(memory_space=pltpu.VMEM)
    smem = pl.BlockSpec(memory_space=pltpu.SMEM)
    several = isinstance(out_shape, list)
    return pl.pallas_call(
        body,
        out_shape=out_shape,
        in_specs=[smem] * len(scalars)
        + [vmem] * (len(arrays) - len(large))
        + [pl.BlockSpec(memory_space=pl.ANY)] * (len(large) + len(after)),
        out_specs=[vmem] * (len(out_shape) - large_outs)
        + [pl.BlockSpec(memory_space=pl.ANY)] * large_outs
        if several
        else vmem,
        scratch_shapes=[pltpu.VMEM(shape, jnp.float32) for shape in scratch]
        + [pltpu.SemaphoreType.DMA((len(scratch),))] * bool(large),
        compiler_params=pltpu.CompilerParams(vmem_limit_bytes=40 << 20),
        cost_estimate=pl.CostEstimate(flops=int(cost * 1e9), bytes_accessed=int(cost * 3e6), transcendentals=0),
    )(*scalars, *arrays, *after)


def shape(*dims, dtype=jnp.float32):
    return jax.ShapeDtypeStruct(dims, dtype)


def strips(kernel, width, place, cost, *arrays, extra=(), **options):
    panel = arrays[0].shape[1]
    outs = [shape(4, panel // 16, width)] * 4
    return kernel_call(kernel, [place], [*outs, *extra], [(panel, width)], cost, *arrays, **options)


def sum_along(values, swapped):
    total = values[0]
    for step in (1, 3, 2):
        total += lax.ppermute(values[step], ("pts", "lm"), plane_step(step, swapped))
    return total


def per_device(kernel_features, factor, diag_inverse, block_order):
    own = kernel_features
    points, panel = own.shape
    half, thin, part = points // 2, panel // 2, panel // 32
    i, j = lax.axis_index("pts"), lax.axis_index("lm")
    chip, core = j // 2, j % 2
    high, x, y = i // 16, (i // 4) % 4, i % 4
    first_core = core == 0
    place = jnp.stack(
        [core, chip, jnp.where(first_core, x, y), jnp.where(first_core, y, x), j, i // 8]
    ).astype(jnp.int32)
    order = block_order

    pair = lax.ppermute(own, "lm", OTHER_CORE)
    sent = lax.dynamic_slice_in_dim(own, (1 - chip) * half, half)
    across = [lax.ppermute(sent[:, at : at + w], "lm", OTHER_CHIP) for at, w in PIECES]

    product = kernel_call(
        near_kernel, [place], shape(panel, panel + thin), [], COSTS[0], own, pair
    )
    widths = [panel + thin + 2 * PIECES[0][1], 2 * PIECES[1][1]]
    early = strips(across_kernel, widths[0], place, COSTS[1], own, pair, across[0], product)
    early_sum = sum_along(early, False)
    late = strips(across_kernel, widths[1], place, COSTS[3], own, pair, across[1], after=(early_sum,))
    late_sum = sum_along(late, False)
    parts = [jnp.concatenate([a, b], -1) for a, b in zip(early_sum, late_sum)]
    inverse = diag_inverse[0]
    near, near_low, far, far_low = kernel_call(
        inverse_kernel,
        [place],
        [shape(2 * panel, panel, dtype=jnp.bfloat16)] * 4,
        [(2 * panel, panel), (2 * panel, panel), (panel, panel)],
        COSTS[2],
        inverse,
        lax.ppermute(inverse, "lm", OTHER_CORE),
        large=(factor, lax.ppermute(factor[: 2 * panel], "lm", OTHER_CORE)),
        after=(early[0],),
    )
    parts, far_low = lax.optimization_barrier((parts, far_low))
    mine = sum_along(parts, True)
    here, there = lax.optimization_barrier(
        tuple(lax.dynamic_slice_in_dim(mine, at * part, part) for at in (high, 1 - high))
    )
    far_here = lax.ppermute(here, "lm", OTHER_CHIP)
    far_there = lax.ppermute(there, ("pts", "lm"), other_high(2))
    here += lax.ppermute(there, ("pts", "lm"), other_high(0))
    away = far_here + far_there

    def spread(value, away):
        return value, away, lax.ppermute(jnp.stack([value, away]), "lm", OTHER_CORE)

    def hop(value):
        got = lax.ppermute(value, "lm", OTHER_CHIP)
        return value, got, lax.ppermute(got, "lm", OTHER_CORE), far, far_low

    def flipped(packed, *kinds):
        got = lax.all_to_all(packed, "pts", 0, 0, axis_index_groups=EIGHTS, tiled=True)
        return [lax.ppermute(got, ("pts", "lm"), swap(k)) for k in kinds]

    square, packed = shape(ROWS, panel), shape(8, 32, 2 * ROWS)
    flops = 2
    width = here.shape[1]
    value = kernel_call(
        first_kernel,
        [place, order],
        square,
        [(4, part, width), (ROWS, 4 * panel), (ROWS, 2 * panel)],
        flops,
        *spread(here, away),
        near,
        near_low,
    )
    _, value = kernel_call(second_kernel, [place], [square, packed], [], flops, *hop(value))
    value = kernel_call(
        third_kernel,
        [place, order],
        square,
        [(4, 8, 32, 2 * ROWS), (2 * panel, 2 * ROWS), (2 * panel, 2 * ROWS)],
        flops,
        *spread(*flipped(value, 0, 2)),
        near,
        near_low,
    )
    result, value = kernel_call(second_kernel, [place], [square, packed], [], flops, *hop(value))
    scale = jnp.full((1,), 1.0 / (points * lax.axis_size("pts")), jnp.float32)
    return kernel_call(
        last_kernel, [place, scale], square, [(panel, 2 * ROWS)], 0, result, *flipped(value, 0)
    )


def solution(mesh):
    placed = (P("pts", "lm"), P(None, "lm"), P("lm", None, None), P())
    return jax.shard_map(
        per_device, mesh=mesh, in_specs=placed, out_specs=P("pts", "lm"), check_vma=False
    )
```

```python
import jax
import jax.numpy as jnp
from jax import lax
from jax.experimental import pallas as pl
from jax.experimental.pallas import tpu as pltpu
from jax.sharding import PartitionSpec as P

PANEL = 512
CLUSTER = 128
COSTS = (40, 6, 4, 4)
PIECES = ((0, 128), (128, 384))
ROWS = 64

CELLS = [(zh, x, y) for zh in range(2) for x in range(4) for y in range(4)]


def pts_index(zh, x, y):
    return (zh * 4 + x) * 4 + y


def plane_step(step, swapped):
    pairs = []
    for z, x, y in CELLS:
        for j in range(4):
            if (j % 2 == 0) != swapped:
                to = pts_index(z, (x + step) % 4, y)
            else:
                to = pts_index(z, x, (y + step) % 4)
            pairs.append((pts_index(z, x, y) * 4 + j, to * 4 + j))
    return pairs


def other_high(k):
    return [
        (pts_index(z, x, y) * 4 + j, pts_index(1 - z, x, y) * 4 + (j ^ k))
        for z, x, y in CELLS
        for j in range(4)
    ]


OTHER_CHIP = [(k, k ^ 2) for k in range(4)]
OTHER_CORE = [(k, k ^ 1) for k in range(4)]


def turn_groups():
    rows = [((a, j), (j, a)) for a in range(4) for j in range(a + 1, 4)]
    rows += [((a, a), (a + 1, a + 1)) for a in (0, 2)]
    return [[(8 * a + b) * 4 + j for a, j in pair for b in range(8)] for pair in rows]


def halves(value):
    first = value.astype(jnp.bfloat16)
    return first, (value - first.astype(jnp.float32)).astype(jnp.bfloat16)


def contract(a, b):
    def one(u, v):
        return lax.dot_general(u, v, (((0,), (0,)), ((), ())), preferred_element_type=jnp.float32)

    return one(a[0], b[0]) + (one(a[0], b[1]) + one(a[1], b[0]))


def multiply(a, b):
    def one(u, v):
        return jnp.dot(u, v, preferred_element_type=jnp.float32)

    return one(a[0], b[0]) + (one(a[0], b[1]) + one(a[1], b[0]))


def write_strips(place, product, outs):
    core, first, second = place[0], place[2], place[3]
    for k in range(4):
        for m in range(4):
            f, g = (first + k) % 4, (second + m) % 4
            strip = jnp.where(core == 0, 4 * f + g, 4 * g + f)
            outs[k][m] = product[pl.ds(pl.multiple_of(strip * 32, 32), 32), :]


def near_kernel(place, own, pair, product):
    panel = own.shape[1]
    thin = panel // 2
    a = halves(own[...])
    product[:, :panel] = contract(a, a) * 0.5

    @pl.when(place[0] == 0)
    def _():
        product[:, panel:] = contract(a, halves(pair[:, :thin]))

    @pl.when(place[0] != 0)
    def _():
        b = [part[:, thin:] for part in a]
        product[:, panel:] = contract(halves(pair[...]), b)


def across_kernel(place, own, pair, value, *refs):
    *others, out0, out1, out2, out3, product = refs
    half, width = value.shape
    rows = pl.ds(pl.multiple_of(place[1] * half, half), half)
    b = halves(value[...])
    start = product.shape[1] - 2 * width
    for other in others:
        product[:, :start] = other[...]
    product[:, start : start + width] = contract(halves(own[rows, :]), b)
    product[:, start + width :] = contract(halves(pair[rows, :]), b)
    write_strips(place, product, (out0, out1, out2, out3))


def inverse_kernel(
    place, inverse, pair_inverse, factor, pair_factor, near, near_low, far, far_low, above, pair_above, link, done
):
    panel = inverse.shape[0]
    start = pl.multiple_of(place[1] * 2 * panel, 2 * panel)
    copies = [
        pltpu.make_async_copy(factor.at[pl.ds(0, 2 * panel), :], above, done.at[0]),
        pltpu.make_async_copy(pair_factor.at[pl.ds(0, 2 * panel), :], pair_above, done.at[1]),
        pltpu.make_async_copy(factor.at[pl.ds(start, panel), :], link, done.at[2]),
    ]
    for copy in copies:
        copy.start()
    for copy in copies:
        copy.wait()
    d = halves(inverse[...])

    def put(high, low, rows, value):
        parts = halves(value)
        high[rows, :] = parts[0]
        low[rows, :] = parts[1]

    top, bottom = slice(0, panel), slice(panel, 2 * panel)

    @pl.when(place[0] == 0)
    def _():
        near[top, :], near_low[top, :] = d
        near[bottom, :] = jnp.zeros_like(d[0])
        near_low[bottom, :] = jnp.zeros_like(d[0])
        for rows in (top, bottom):
            put(far, far_low, rows, multiply(halves(above[rows, :]), d))

    @pl.when(place[0] != 0)
    def _():
        near[bottom, :], near_low[bottom, :] = d
        corner = -multiply(halves(pair_inverse[...]), halves(multiply(halves(link[...]), d)))
        put(near, near_low, top, corner)
        c = halves(corner)
        for rows in (top, bottom):
            value = multiply(halves(above[rows, :]), d) + multiply(halves(pair_above[rows, :]), c)
            put(far, far_low, rows, value)


def collect(place, held, value, far, other):
    j = place[4]
    held[j] = value[...]
    held[j ^ 2] = far[...]
    held[j ^ 1] = other[0]
    held[j ^ 3] = other[1]


def first_kernel(place, order, value, far, other, near, near_low, out, held, upper, ordered):
    part = value.shape[0]
    panel = near.shape[1]
    thin = panel // 2
    collect(place, held, value, far, other)

    def put(q, column, source, first, width):
        upper[part * q : part * (q + 1), column : column + width] = held[
            source, :, first : first + width
        ]

    for q in range(4):
        chip, core = divmod(q, 2)
        put(q, q * panel, q, 0, panel)
        if core == 0:
            put(q, (q + 1) * panel, q, panel, thin)
            put(q, (q + 1) * panel + thin, q + 1, panel, thin)
        else:
            upper[part * q : part * (q + 1), (q - 1) * panel : q * panel] = jnp.zeros(
                (part, panel), jnp.float32
            )
        for c in range(2):
            first = panel + thin
            for at, width in PIECES:
                column = (2 * (1 - chip) + c) * panel + at
                put(q, column, q if c != core else q ^ 1, first + width * (c == core), width)
                first += 2 * width
    for k in range(8):
        block = order[place[1] * 8 + k]
        ordered[:, k * CLUSTER : (k + 1) * CLUSTER] = upper[
            :, pl.ds(pl.multiple_of(block * CLUSTER, CLUSTER), CLUSTER)
        ]
    out[...] = multiply(halves(ordered[...]), (near[...], near_low[...]))


def less_far(place, value, got, got_pair, far, far_low, solved):
    panel = value.shape[1]
    solved[...] = value[...]

    @pl.when(place[1] != 0)
    def _():
        core = place[0]
        rows = [pl.ds(pl.multiple_of(c * panel, panel), panel) for c in (core, 1 - core)]
        total = value[...]
        for source, r in zip((got, got_pair), rows):
            total -= multiply(halves(source[...]), (far[r, :], far_low[r, :]))
        solved[...] = total


def pack(row, solved, out):
    out[...] = jnp.zeros(out.shape, out.dtype)
    left = lax.broadcasted_iota(jnp.int32, (32, 2 * ROWS), 1) < ROWS
    for g in range(4):
        low = solved[:32, g * 2 * ROWS : (g + 1) * 2 * ROWS]
        high = solved[32:, g * 2 * ROWS : (g + 1) * 2 * ROWS]
        out[8 * row + 2 * g] = jnp.where(left, low, pltpu.roll(high, ROWS, 1))
        out[8 * row + 2 * g + 1] = jnp.where(left, pltpu.roll(low, ROWS, 1), high)


def second_kernel(place, value, got, got_pair, far, far_low, solved, out):
    less_far(place, value, got, got_pair, far, far_low, solved)
    pack(place[6], solved, out)


def third_kernel(place, order, value, far, other, near, near_low, out, held, rows, ordered):
    part = value.shape[1] // 2
    collect(place, held, value, far, other)
    for a in range(4):
        for b in range(8):
            high, strip = a // 2, 8 * (a % 2) + b
            for q in range(2):
                start = 512 * q + 32 * strip + part * high
                rows[start : start + part, :] = held[a, b, part * q : part * (q + 1), :]
    for k in range(8):
        block = order[place[1] * 8 + k]
        taken = rows[pl.ds(pl.multiple_of((block % 8) * CLUSTER, CLUSTER), CLUSTER), :]
        ordered[k * CLUSTER : (k + 1) * CLUSTER, :] = jnp.where(
            block >= 8, pltpu.roll(taken, ROWS, 1), taken
        )
    out[...] = contract(halves(ordered[...]), (near[...], near_low[...]))[:ROWS]


def last_kernel(place, scale, result, turned, out, rows):
    for b in range(8):
        block = turned[8 * place[6] + b]
        rows[64 * b : 64 * b + 32, :] = block
        rows[64 * b + 32 : 64 * b + 64, :] = pltpu.roll(block, ROWS, 1)
    both = (result[...] + rows[...].T[:ROWS]) * scale[0]
    out[...] = jnp.where(place[5] <= place[4], both, 0.0)


def kernel_call(kernel, scalars, out_shape, scratch, cost, *arrays, after=(), large=(), large_outs=0):
    arrays = (*arrays, *large)
    inputs = len(scalars) + len(arrays)

    def body(*refs):
        kernel(*refs[:inputs], *refs[inputs + len(after) :])

    vmem = pl.BlockSpec(memory_space=pltpu.VMEM)
    smem = pl.BlockSpec(memory_space=pltpu.SMEM)
    several = isinstance(out_shape, list)
    return pl.pallas_call(
        body,
        out_shape=out_shape,
        in_specs=[smem] * len(scalars)
        + [vmem] * (len(arrays) - len(large))
        + [pl.BlockSpec(memory_space=pl.ANY)] * (len(large) + len(after)),
        out_specs=[vmem] * (len(out_shape) - large_outs)
        + [pl.BlockSpec(memory_space=pl.ANY)] * large_outs
        if several
        else vmem,
        scratch_shapes=[pltpu.VMEM(shape, jnp.float32) for shape in scratch]
        + [pltpu.SemaphoreType.DMA((len(scratch),))] * bool(large),
        compiler_params=pltpu.CompilerParams(vmem_limit_bytes=40 << 20),
        cost_estimate=pl.CostEstimate(flops=int(cost * 1e9), bytes_accessed=int(cost * 3e6), transcendentals=0),
    )(*scalars, *arrays, *after)


def shape(*dims, dtype=jnp.float32):
    return jax.ShapeDtypeStruct(dims, dtype)


def strips(kernel, width, place, cost, *arrays, extra=(), **options):
    panel = arrays[0].shape[1]
    outs = [shape(4, panel // 16, width)] * 4
    return kernel_call(kernel, [place], [*outs, *extra], [(panel, width)], cost, *arrays, **options)


def sum_along(values, swapped):
    total = values[0]
    for step in (1, 3, 2):
        total += lax.ppermute(values[step], ("pts", "lm"), plane_step(step, swapped))
    return total


def per_device(kernel_features, factor, diag_inverse, block_order):
    own = kernel_features
    points, panel = own.shape
    half, thin, part = points // 2, panel // 2, panel // 32
    i, j = lax.axis_index("pts"), lax.axis_index("lm")
    chip, core = j // 2, j % 2
    high, x, y = i // 16, (i // 4) % 4, i % 4
    first_core = core == 0
    group = i // 8
    row = jnp.where(group < j, 1, jnp.where(group > j, 0, j % 2))
    place = jnp.stack(
        [core, chip, jnp.where(first_core, x, y), jnp.where(first_core, y, x), j, group, row]
    ).astype(jnp.int32)
    order = block_order

    pair = lax.ppermute(own, "lm", OTHER_CORE)
    sent = lax.dynamic_slice_in_dim(own, (1 - chip) * half, half)
    across = [lax.ppermute(sent[:, at : at + w], "lm", OTHER_CHIP) for at, w in PIECES]
    across = [lax.ppermute(value, "lm", OTHER_CORE) for value in across]

    product = kernel_call(
        near_kernel, [place], shape(panel, panel + thin), [], COSTS[0], own, pair
    )
    widths = [panel + thin + 2 * PIECES[0][1], 2 * PIECES[1][1]]
    early = strips(across_kernel, widths[0], place, COSTS[1], own, pair, across[0], product)
    early_sum = sum_along(early, False)
    late = strips(across_kernel, widths[1], place, COSTS[3], own, pair, across[1], after=(early_sum,))
    late_sum = sum_along(late, False)
    parts = [jnp.concatenate([a, b], -1) for a, b in zip(early_sum, late_sum)]
    inverse = diag_inverse[0]
    near, near_low, far, far_low = kernel_call(
        inverse_kernel,
        [place],
        [shape(2 * panel, panel, dtype=jnp.bfloat16)] * 4,
        [(2 * panel, panel), (2 * panel, panel), (panel, panel)],
        COSTS[2],
        inverse,
        lax.ppermute(inverse, "lm", OTHER_CORE),
        large=(factor, lax.ppermute(factor[: 2 * panel], "lm", OTHER_CORE)),
        after=(early[0],),
    )
    parts, far_low = lax.optimization_barrier((parts, far_low))
    mine = sum_along(parts, True)
    here, there = lax.optimization_barrier(
        tuple(lax.dynamic_slice_in_dim(mine, at * part, part) for at in (high, 1 - high))
    )
    far_here = lax.ppermute(here, "lm", OTHER_CHIP)
    far_there = lax.ppermute(there, ("pts", "lm"), other_high(2))
    here += lax.ppermute(there, ("pts", "lm"), other_high(0))
    away = far_here + far_there

    def spread(value, away):
        return value, away, lax.ppermute(jnp.stack([value, away]), "lm", OTHER_CORE)

    def hop(value):
        got = lax.ppermute(value, "lm", OTHER_CHIP)
        return value, got, lax.ppermute(got, "lm", OTHER_CORE), far, far_low

    def turned(packed):
        groups = turn_groups()
        return lax.all_to_all(packed, ("pts", "lm"), 0, 0, axis_index_groups=groups, tiled=True)

    square, packed = shape(ROWS, panel), shape(16, 32, 2 * ROWS)
    flops = 2
    width = here.shape[1]
    value = kernel_call(
        first_kernel,
        [place, order],
        square,
        [(4, part, width), (ROWS, 4 * panel), (ROWS, 2 * panel)],
        flops,
        *spread(here, away),
        near,
        near_low,
    )
    _, value = kernel_call(second_kernel, [place], [square, packed], [], flops, *hop(value))
    value = lax.dynamic_slice_in_dim(turned(value), 8 * row, 8)
    away = lax.ppermute(value, "lm", OTHER_CHIP)
    value = kernel_call(
        third_kernel,
        [place, order],
        square,
        [(4, 8, 32, 2 * ROWS), (2 * panel, 2 * ROWS), (2 * panel, 2 * ROWS)],
        flops,
        *spread(value, away),
        near,
        near_low,
    )
    result, value = kernel_call(second_kernel, [place], [square, packed], [], flops, *hop(value))
    scale = jnp.full((1,), 1.0 / (points * lax.axis_size("pts")), jnp.float32)
    return kernel_call(
        last_kernel, [place, scale], square, [(panel, 2 * ROWS)], 0, result, turned(value)
    )


def solution(mesh):
    placed = (P("pts", "lm"), P(None, "lm"), P("lm", None, None), P())
    return jax.shard_map(
        per_device, mesh=mesh, in_specs=placed, out_specs=P("pts", "lm"), check_vma=False
    )
```

```python
import jax
import jax.numpy as jnp
from jax import lax
from jax.experimental import pallas as pl
from jax.experimental.pallas import tpu as pltpu
from jax.sharding import PartitionSpec as P

PANEL = 512
CLUSTER = 128
COSTS = (40, 6, 4, 4)
PIECES = ((0, 128), (128, 384))
ROWS = 64
KEPT = 3 * CLUSTER

CELLS = [(zh, x, y) for zh in range(2) for x in range(4) for y in range(4)]


def pts_index(zh, x, y):
    return (zh * 4 + x) * 4 + y


def plane_step(step, swapped):
    pairs = []
    for z, x, y in CELLS:
        for j in range(4):
            if (j % 2 == 0) != swapped:
                to = pts_index(z, (x + step) % 4, y)
            else:
                to = pts_index(z, x, (y + step) % 4)
            pairs.append((pts_index(z, x, y) * 4 + j, to * 4 + j))
    return pairs


def other_high(k):
    return [
        (pts_index(z, x, y) * 4 + j, pts_index(1 - z, x, y) * 4 + (j ^ k))
        for z, x, y in CELLS
        for j in range(4)
    ]


OTHER_CHIP = [(k, k ^ 2) for k in range(4)]
OTHER_CORE = [(k, k ^ 1) for k in range(4)]


def turn_groups():
    rows = [((a, j), (j, a)) for a in range(4) for j in range(a + 1, 4)]
    rows += [((a, a), (a + 1, a + 1)) for a in (0, 2)]
    return [[(8 * a + b) * 4 + j for a, j in pair for b in range(8)] for pair in rows]


def halves(value):
    first = value.astype(jnp.bfloat16)
    return first, (value - first.astype(jnp.float32)).astype(jnp.bfloat16)


def contract(a, b):
    def one(u, v):
        return lax.dot_general(u, v, (((0,), (0,)), ((), ())), preferred_element_type=jnp.float32)

    return one(a[0], b[0]) + (one(a[0], b[1]) + one(a[1], b[0]))


def multiply(a, b):
    def one(u, v):
        return jnp.dot(u, v, preferred_element_type=jnp.float32)

    rows = a[0].shape[0]
    both = one(jnp.concatenate(a, 0), b[0])
    return both[:rows] + (both[rows:] + one(a[0], b[1]))


def write_strips(place, product, outs, wrapped=0):
    core, first, second = place[0], place[2], place[3]
    kept = KEPT if wrapped else 0
    if wrapped:
        block = lax.broadcasted_iota(jnp.int32, (32, KEPT), 1) // CLUSTER
        weight = jnp.where(block == 1, 1.0, 0.5)
    for k in range(4):
        for m in range(4):
            f, g = (first + k) % 4, (second + m) % 4
            strip = jnp.where(core == 0, 4 * f + g, 4 * g + f)
            rows = pl.ds(pl.multiple_of(strip * 32, 32), 32)
            if wrapped:
                start = jnp.where(core == 0, f, g) * CLUSTER
                columns = pl.ds(pl.multiple_of(start, CLUSTER), KEPT)
                outs[k][m, :, :KEPT] = product[rows, columns] * weight
            outs[k][m, :, kept:] = product[rows, wrapped:]


def near_kernel(place, own, pair, product):
    panel = own.shape[1]
    thin = panel // 2
    a = halves(own[...])
    product[:, :panel] = contract(a, a)

    @pl.when(place[0] == 0)
    def _():
        product[:, panel:] = contract(a, halves(pair[:, :thin]))

    @pl.when(place[0] != 0)
    def _():
        b = [part[:, thin:] for part in a]
        product[:, panel:] = contract(halves(pair[...]), b)


def early_kernel(place, own, pair, value, other, out0, out1, out2, out3, product):
    half, width = value.shape
    panel = own.shape[1]
    rows = pl.ds(pl.multiple_of(place[1] * half, half), half)
    b = halves(value[...])
    again = panel + 2 * CLUSTER
    product[:, :panel] = other[:, :panel]
    product[:, panel:again] = other[:, : 2 * CLUSTER]
    start = again + other.shape[1] - panel
    product[:, again:start] = other[:, panel:]
    product[:, start : start + width] = contract(halves(own[rows, :]), b)
    product[:, start + width :] = contract(halves(pair[rows, :]), b)
    write_strips(place, product, (out0, out1, out2, out3), again)


def prepare_kernel(place, own, pair, first, second):
    panel, half = own.shape[1], own.shape[0] // 2
    rows = pl.ds(pl.multiple_of(place[1] * half, half), half)
    for k, panel_of in enumerate((own, pair)):
        into = slice(k * panel, (k + 1) * panel)
        first[into, :], second[into, :] = halves(panel_of[rows, :].T)


def late_kernel(place, first, second, value, out0, out1, out2, out3, product):
    panel, width = first.shape[0] // 2, value.shape[1]
    b = halves(value[...])
    for k in range(2):
        rows = slice(k * panel, (k + 1) * panel)
        product[:, k * width : (k + 1) * width] = multiply((first[rows, :], second[rows, :]), b)
    write_strips(place, product, (out0, out1, out2, out3))


def inverse_kernel(
    place, inverse, pair_inverse, factor, pair_factor, near, near_low, far, far_low, above, pair_above, link, done
):
    panel = inverse.shape[0]
    start = pl.multiple_of(place[1] * 2 * panel, 2 * panel)
    copies = [
        pltpu.make_async_copy(factor.at[pl.ds(0, 2 * panel), :], above, done.at[0]),
        pltpu.make_async_copy(pair_factor.at[pl.ds(0, 2 * panel), :], pair_above, done.at[1]),
        pltpu.make_async_copy(factor.at[pl.ds(start, panel), :], link, done.at[2]),
    ]
    for copy in copies:
        copy.start()
    for copy in copies:
        copy.wait()
    d = halves(inverse[...])

    def put(high, low, rows, value):
        parts = halves(value)
        high[rows, :] = parts[0]
        low[rows, :] = parts[1]

    top, bottom = slice(0, panel), slice(panel, 2 * panel)

    @pl.when(place[0] == 0)
    def _():
        near[top, :], near_low[top, :] = d
        near[bottom, :] = jnp.zeros_like(d[0])
        near_low[bottom, :] = jnp.zeros_like(d[0])
        for rows in (top, bottom):
            put(far, far_low, rows, multiply(halves(above[rows, :]), d))

    @pl.when(place[0] != 0)
    def _():
        near[bottom, :], near_low[bottom, :] = d
        corner = -multiply(halves(pair_inverse[...]), halves(multiply(halves(link[...]), d)))
        put(near, near_low, top, corner)
        c = halves(corner)
        for rows in (top, bottom):
            value = multiply(halves(above[rows, :]), d) + multiply(halves(pair_above[rows, :]), c)
            put(far, far_low, rows, value)


def collect(place, held, value, far, other):
    j = place[4]
    held[j] = value[...]
    held[j ^ 2] = far[...]
    held[j ^ 1] = other[0]
    held[j ^ 3] = other[1]


def first_kernel(place, order, value, far, other, near, near_low, out, held, upper, ordered):
    part = value.shape[0]
    panel = near.shape[1]
    thin = panel // 2
    collect(place, held, value, far, other)

    def put(q, column, source, first, width):
        upper[part * q : part * (q + 1), column : column + width] = held[
            source, :, first : first + width
        ]

    nothing = jnp.zeros((part, CLUSTER), jnp.float32)
    for q in range(4):
        chip, core = divmod(q, 2)
        for t in range(4):
            start = q * panel + (place[7] + t) % 4 * CLUSTER
            columns = pl.ds(pl.multiple_of(start, CLUSTER), CLUSTER)
            kept = held[q, :, t * CLUSTER : (t + 1) * CLUSTER] if t < 3 else nothing
            upper[part * q : part * (q + 1), columns] = kept
        if core == 0:
            put(q, (q + 1) * panel, q, KEPT, thin)
            put(q, (q + 1) * panel + thin, q + 1, KEPT, thin)
        else:
            upper[part * q : part * (q + 1), (q - 1) * panel : q * panel] = jnp.zeros(
                (part, panel), jnp.float32
            )
        for c in range(2):
            first = KEPT + thin
            for (at, width), straight in zip(PIECES, (c == core, c != core)):
                column = (2 * (1 - chip) + c) * panel + at
                put(q, column, q if straight else q ^ 1, first + width * (not straight), width)
                first += 2 * width
    for k in range(8):
        block = order[place[1] * 8 + k]
        ordered[:, k * CLUSTER : (k + 1) * CLUSTER] = upper[
            :, pl.ds(pl.multiple_of(block * CLUSTER, CLUSTER), CLUSTER)
        ]
    out[...] = multiply(halves(ordered[...]), (near[...], near_low[...]))


def less_far(place, value, got, got_pair, far, far_low, solved):
    panel = value.shape[1]
    solved[...] = value[...]

    @pl.when(place[1] != 0)
    def _():
        core = place[0]
        rows = [pl.ds(pl.multiple_of(c * panel, panel), panel) for c in (core, 1 - core)]
        total = value[...]
        for source, r in zip((got, got_pair), rows):
            total -= multiply(halves(source[...]), (far[r, :], far_low[r, :]))
        solved[...] = total


def pack(row, solved, out):
    out[...] = jnp.zeros(out.shape, out.dtype)
    left = lax.broadcasted_iota(jnp.int32, (32, 2 * ROWS), 1) < ROWS
    for g in range(4):
        low = solved[:32, g * 2 * ROWS : (g + 1) * 2 * ROWS]
        high = solved[32:, g * 2 * ROWS : (g + 1) * 2 * ROWS]
        out[8 * row + 2 * g] = jnp.where(left, low, pltpu.roll(high, ROWS, 1))
        out[8 * row + 2 * g + 1] = jnp.where(left, pltpu.roll(low, ROWS, 1), high)


def second_kernel(place, value, got, got_pair, far, far_low, solved, out):
    less_far(place, value, got, got_pair, far, far_low, solved)
    pack(place[6], solved, out)


def third_kernel(place, order, value, far, other, near, near_low, out, held, rows, ordered):
    part = value.shape[1] // 2
    collect(place, held, value, far, other)
    for a in range(4):
        for b in range(8):
            high, strip = a // 2, 8 * (a % 2) + b
            for q in range(2):
                start = 512 * q + 32 * strip + part * high
                rows[start : start + part, :] = held[a, b, part * q : part * (q + 1), :]
    for k in range(8):
        block = order[place[1] * 8 + k]
        taken = rows[pl.ds(pl.multiple_of((block % 8) * CLUSTER, CLUSTER), CLUSTER), :]
        ordered[k * CLUSTER : (k + 1) * CLUSTER, :] = jnp.where(
            block >= 8, pltpu.roll(taken, ROWS, 1), taken
        )
    first, second = halves(ordered[...])
    left = lax.broadcasted_iota(jnp.int32, ordered.shape, 1) < ROWS
    beside = pltpu.roll(second.astype(jnp.float32), ROWS, 1)
    beside = jnp.where(left, first.astype(jnp.float32), beside).astype(jnp.bfloat16)

    def one(u, v):
        return lax.dot_general(u, v, (((0,), (0,)), ((), ())), preferred_element_type=jnp.float32)

    both = one(beside, near[...])
    out[...] = both[:ROWS] + (both[ROWS:] + one(first, near_low[...])[:ROWS])


def last_kernel(place, scale, result, turned, out, rows):
    for b in range(8):
        block = turned[8 * place[6] + b]
        rows[64 * b : 64 * b + 32, :] = block
        rows[64 * b + 32 : 64 * b + 64, :] = pltpu.roll(block, ROWS, 1)
    both = (result[...] + rows[...].T[:ROWS]) * scale[0]
    out[...] = jnp.where(place[5] <= place[4], both, 0.0)


def kernel_call(kernel, scalars, out_shape, scratch, cost, *arrays, after=(), large=(), large_outs=0):
    arrays = (*arrays, *large)
    inputs = len(scalars) + len(arrays)

    def body(*refs):
        kernel(*refs[:inputs], *refs[inputs + len(after) :])

    vmem = pl.BlockSpec(memory_space=pltpu.VMEM)
    smem = pl.BlockSpec(memory_space=pltpu.SMEM)
    several = isinstance(out_shape, list)
    return pl.pallas_call(
        body,
        out_shape=out_shape,
        in_specs=[smem] * len(scalars)
        + [vmem] * (len(arrays) - len(large))
        + [pl.BlockSpec(memory_space=pl.ANY)] * (len(large) + len(after)),
        out_specs=[vmem] * (len(out_shape) - large_outs)
        + [pl.BlockSpec(memory_space=pl.ANY)] * large_outs
        if several
        else vmem,
        scratch_shapes=[pltpu.VMEM(shape, jnp.float32) for shape in scratch]
        + [pltpu.SemaphoreType.DMA((len(scratch),))] * bool(large),
        compiler_params=pltpu.CompilerParams(vmem_limit_bytes=40 << 20),
        cost_estimate=pl.CostEstimate(flops=int(cost * 1e9), bytes_accessed=int(cost * 3e6), transcendentals=0),
    )(*scalars, *arrays, *after)


def shape(*dims, dtype=jnp.float32):
    return jax.ShapeDtypeStruct(dims, dtype)


def sum_along(values, swapped):
    got = [
        lax.ppermute(values[step], ("pts", "lm"), plane_step(step, swapped)) for step in (1, 3, 2)
    ]
    return values[0] + got[0] + got[1] + got[2], got


def per_device(kernel_features, factor, diag_inverse, block_order):
    own = kernel_features
    points, panel = own.shape
    half, thin, part = points // 2, panel // 2, panel // 32
    i, j = lax.axis_index("pts"), lax.axis_index("lm")
    chip, core = j // 2, j % 2
    high, x, y = i // 16, (i // 4) % 4, i % 4
    first_core = core == 0
    group = i // 8
    row = jnp.where(group < j, 1, jnp.where(group > j, 0, j % 2))
    place = jnp.stack(
        [core, chip, jnp.where(first_core, x, y), jnp.where(first_core, y, x), j, group, row, x]
    ).astype(jnp.int32)
    order = block_order

    pair = lax.ppermute(own, "lm", OTHER_CORE)
    sent = lax.dynamic_slice_in_dim(own, (1 - chip) * half, half)
    across = [sent[:, at : at + w] for at, w in PIECES]
    pair, across[1] = lax.optimization_barrier((pair, across[1]))
    across = [lax.ppermute(value, "lm", OTHER_CHIP) for value in across]

    product = kernel_call(
        near_kernel, [place], shape(panel, panel + thin), [], COSTS[0], own, pair
    )
    widths = [KEPT + thin + 2 * PIECES[0][1], 2 * PIECES[1][1]]
    early = kernel_call(
        early_kernel,
        [place],
        [shape(4, panel // 16, widths[0])] * 4,
        [(panel, panel + 2 * CLUSTER + thin + 2 * PIECES[0][1])],
        COSTS[1],
        own,
        pair,
        across[0],
        product,
    )
    early_sum, arrived = sum_along(early, False)
    prepared = kernel_call(
        prepare_kernel,
        [place],
        [shape(2 * panel, half, dtype=jnp.bfloat16)] * 2,
        [],
        COSTS[3],
        own,
        pair,
        after=(early[0],),
    )
    across[1], *prepared_and = lax.optimization_barrier((across[1], *prepared, *arrived))
    prepared = prepared_and[:2]
    across[1] = lax.ppermute(across[1], "lm", OTHER_CORE)
    late = kernel_call(
        late_kernel,
        [place],
        [shape(4, panel // 16, widths[1])] * 4,
        [(panel, widths[1])],
        COSTS[3],
        *prepared,
        across[1],
        after=(early_sum,),
    )
    late_sum, _ = sum_along(late, False)
    parts = [jnp.concatenate([a, b], -1) for a, b in zip(early_sum, late_sum)]
    inverse = diag_inverse[0]
    near, near_low, far, far_low = kernel_call(
        inverse_kernel,
        [place],
        [shape(2 * panel, panel, dtype=jnp.bfloat16)] * 4,
        [(2 * panel, panel), (2 * panel, panel), (panel, panel)],
        COSTS[2],
        inverse,
        lax.ppermute(inverse, "lm", OTHER_CORE),
        large=(factor, lax.ppermute(factor[: 2 * panel], "lm", OTHER_CORE)),
        after=(early[0],),
    )
    parts, far_low = lax.optimization_barrier((parts, far_low))
    mine, _ = sum_along(parts, True)
    here, there = lax.optimization_barrier(
        tuple(lax.dynamic_slice_in_dim(mine, at * part, part) for at in (high, 1 - high))
    )
    far_here = lax.ppermute(here, "lm", OTHER_CHIP)
    far_there = lax.ppermute(there, ("pts", "lm"), other_high(2))
    here += lax.ppermute(there, ("pts", "lm"), other_high(0))
    away = far_here + far_there

    def spread(value, away):
        return value, away, lax.ppermute(jnp.stack([value, away]), "lm", OTHER_CORE)

    def hop(value):
        got = lax.ppermute(value, "lm", OTHER_CHIP)
        return value, got, lax.ppermute(got, "lm", OTHER_CORE), far, far_low

    def turned(packed):
        groups = turn_groups()
        return lax.all_to_all(packed, ("pts", "lm"), 0, 0, axis_index_groups=groups, tiled=True)

    square, packed = shape(ROWS, panel), shape(16, 32, 2 * ROWS)
    flops = 2
    width = here.shape[1]
    value = kernel_call(
        first_kernel,
        [place, order],
        square,
        [(4, part, width), (ROWS, 4 * panel), (ROWS, 2 * panel)],
        flops,
        *spread(here, away),
        near,
        near_low,
    )
    _, value = kernel_call(second_kernel, [place], [square, packed], [], flops, *hop(value))
    value = lax.dynamic_slice_in_dim(turned(value), 8 * row, 8)
    away = lax.ppermute(value, "lm", OTHER_CHIP)
    value = kernel_call(
        third_kernel,
        [place, order],
        square,
        [(4, 8, 32, 2 * ROWS), (2 * panel, 2 * ROWS), (2 * panel, 2 * ROWS)],
        flops,
        *spread(value, away),
        near,
        near_low,
    )
    result, value = kernel_call(second_kernel, [place], [square, packed], [], flops, *hop(value))
    scale = jnp.full((1,), 1.0 / (points * lax.axis_size("pts")), jnp.float32)
    return kernel_call(
        last_kernel, [place, scale], square, [(panel, 2 * ROWS)], 0, result, turned(value)
    )


def solution(mesh):
    placed = (P("pts", "lm"), P(None, "lm"), P("lm", None, None), P())
    return jax.shard_map(
        per_device, mesh=mesh, in_specs=placed, out_specs=P("pts", "lm"), check_vma=False
    )
```

```python
import jax
import jax.numpy as jnp
from jax import lax
from jax.experimental import pallas as pl
from jax.experimental.pallas import tpu as pltpu
from jax.sharding import PartitionSpec as P

PANEL = 512
CLUSTER = 128
COSTS = (40, 6, 4, 4)
PIECES = ((0, 128), (128, 384))
ROWS = 64
KEPT = 3 * CLUSTER

CELLS = [(zh, x, y) for zh in range(2) for x in range(4) for y in range(4)]


def pts_index(zh, x, y):
    return (zh * 4 + x) * 4 + y


def plane_step(step, swapped):
    pairs = []
    for z, x, y in CELLS:
        for j in range(4):
            if (j % 2 == 0) != swapped:
                to = pts_index(z, (x + step) % 4, y)
            else:
                to = pts_index(z, x, (y + step) % 4)
            pairs.append((pts_index(z, x, y) * 4 + j, to * 4 + j))
    return pairs


def other_high(k):
    return [
        (pts_index(z, x, y) * 4 + j, pts_index(1 - z, x, y) * 4 + (j ^ k))
        for z, x, y in CELLS
        for j in range(4)
    ]


OTHER_CHIP = [(k, k ^ 2) for k in range(4)]
OTHER_CORE = [(k, k ^ 1) for k in range(4)]


def turn_groups():
    rows = [((a, j), (j, a)) for a in range(4) for j in range(a + 1, 4)]
    rows += [((a, a), (a + 1, a + 1)) for a in (0, 2)]
    return [[(8 * a + b) * 4 + j for a, j in pair for b in range(8)] for pair in rows]


def halves(value):
    first = value.astype(jnp.bfloat16)
    return first, (value - first.astype(jnp.float32)).astype(jnp.bfloat16)


def contract(a, b):
    def one(u, v):
        return lax.dot_general(u, v, (((0,), (0,)), ((), ())), preferred_element_type=jnp.float32)

    return one(a[0], b[0]) + (one(a[0], b[1]) + one(a[1], b[0]))


def multiply(a, b):
    def one(u, v):
        return jnp.dot(u, v, preferred_element_type=jnp.float32)

    rows = a[0].shape[0]
    both = one(jnp.concatenate(a, 0), b[0])
    return both[:rows] + (both[rows:] + one(a[0], b[1]))


def write_strips(place, product, outs, own_product=None):
    core, first, second = place[0], place[2], place[3]
    start = 0
    if own_product is not None:
        block = lax.broadcasted_iota(jnp.int32, (32, KEPT), 1) // CLUSTER
        weight = jnp.where(block == 1, 1.0, 0.5)
        wrapped = PANEL + 2 * CLUSTER
        start = KEPT + own_product.shape[1] - wrapped
    for k in range(4):
        for m in range(4):
            f, g = (first + k) % 4, (second + m) % 4
            strip = jnp.where(core == 0, 4 * f + g, 4 * g + f)
            rows = pl.ds(pl.multiple_of(strip * 32, 32), 32)
            if own_product is not None:
                at = jnp.where(core == 0, f, g) * CLUSTER
                columns = pl.ds(pl.multiple_of(at, CLUSTER), KEPT)
                outs[k][m, :, :KEPT] = own_product[rows, columns] * weight
                outs[k][m, :, KEPT:start] = own_product[rows, wrapped:]
            outs[k][m, :, start:] = product[rows, :]


def near_kernel(place, own, pair, product):
    panel = own.shape[1]
    thin = panel // 2
    wrapped = panel + 2 * CLUSTER
    a = halves(own[...])
    square = contract(a, a)
    product[:, :panel] = square
    product[:, panel:wrapped] = square[:, : 2 * CLUSTER]

    @pl.when(place[0] == 0)
    def _():
        product[:, wrapped:] = contract(a, halves(pair[:, :thin]))

    @pl.when(place[0] != 0)
    def _():
        b = [part[:, thin:] for part in a]
        product[:, wrapped:] = contract(halves(pair[...]), b)


def early_kernel(place, own, pair, value, own_product, out0, out1, out2, out3, product):
    half, width = value.shape
    rows = pl.ds(pl.multiple_of(place[1] * half, half), half)
    b = halves(value[...])
    product[:, :width] = contract(b, halves(own[rows, :])).T
    product[:, width:] = contract(b, halves(pair[rows, :])).T
    write_strips(place, product, (out0, out1, out2, out3), own_product)


def prepare_kernel(place, own, pair, first, second):
    panel, half = own.shape[1], own.shape[0] // 2
    rows = pl.ds(pl.multiple_of(place[1] * half, half), half)
    for k, panel_of in enumerate((own, pair)):
        into = slice(k * panel, (k + 1) * panel)
        first[into, :], second[into, :] = halves(panel_of[rows, :].T)


def late_kernel(place, first, second, value, out0, out1, out2, out3, product):
    panel, width = first.shape[0] // 2, value.shape[1]
    b = halves(value[...])
    for k in range(2):
        rows = slice(k * panel, (k + 1) * panel)
        product[:, k * width : (k + 1) * width] = multiply((first[rows, :], second[rows, :]), b)
    write_strips(place, product, (out0, out1, out2, out3))


def inverse_kernel(
    place, inverse, pair_inverse, factor, pair_factor, near, near_low, far, far_low, above, pair_above, link, done
):
    panel = inverse.shape[0]
    start = pl.multiple_of(place[1] * 2 * panel, 2 * panel)
    copies = [
        pltpu.make_async_copy(factor.at[pl.ds(0, 2 * panel), :], above, done.at[0]),
        pltpu.make_async_copy(pair_factor.at[pl.ds(0, 2 * panel), :], pair_above, done.at[1]),
        pltpu.make_async_copy(factor.at[pl.ds(start, panel), :], link, done.at[2]),
    ]
    for copy in copies:
        copy.start()
    for copy in copies:
        copy.wait()
    d = halves(inverse[...])

    def put(high, low, rows, value):
        parts = halves(value)
        high[rows, :] = parts[0]
        low[rows, :] = parts[1]

    top, bottom = slice(0, panel), slice(panel, 2 * panel)

    @pl.when(place[0] == 0)
    def _():
        near[top, :], near_low[top, :] = d
        near[bottom, :] = jnp.zeros_like(d[0])
        near_low[bottom, :] = jnp.zeros_like(d[0])
        for rows in (top, bottom):
            put(far, far_low, rows, multiply(halves(above[rows, :]), d))

    @pl.when(place[0] != 0)
    def _():
        near[bottom, :], near_low[bottom, :] = d
        corner = -multiply(halves(pair_inverse[...]), halves(multiply(halves(link[...]), d)))
        put(near, near_low, top, corner)
        c = halves(corner)
        for rows in (top, bottom):
            value = multiply(halves(above[rows, :]), d) + multiply(halves(pair_above[rows, :]), c)
            put(far, far_low, rows, value)


def collect(place, held, value, far, other):
    j = place[4]
    held[j] = value[...]
    held[j ^ 2] = far[...]
    held[j ^ 1] = other[0]
    held[j ^ 3] = other[1]


def first_kernel(place, order, value, far, other, near, near_low, out, held, upper, ordered):
    part = value.shape[0]
    panel = near.shape[1]
    thin = panel // 2
    collect(place, held, value, far, other)

    def put(q, column, source, first, width):
        upper[part * q : part * (q + 1), column : column + width] = held[
            source, :, first : first + width
        ]

    nothing = jnp.zeros((part, CLUSTER), jnp.float32)
    for q in range(4):
        chip, core = divmod(q, 2)
        for t in range(4):
            start = q * panel + (place[7] + t) % 4 * CLUSTER
            columns = pl.ds(pl.multiple_of(start, CLUSTER), CLUSTER)
            kept = held[q, :, t * CLUSTER : (t + 1) * CLUSTER] if t < 3 else nothing
            upper[part * q : part * (q + 1), columns] = kept
        if core == 0:
            put(q, (q + 1) * panel, q, KEPT, thin)
            put(q, (q + 1) * panel + thin, q + 1, KEPT, thin)
        else:
            upper[part * q : part * (q + 1), (q - 1) * panel : q * panel] = jnp.zeros(
                (part, panel), jnp.float32
            )
        for c in range(2):
            first = KEPT + thin
            for (at, width), straight in zip(PIECES, (c == core, c != core)):
                column = (2 * (1 - chip) + c) * panel + at
                put(q, column, q if straight else q ^ 1, first + width * (not straight), width)
                first += 2 * width
    for k in range(8):
        block = order[place[1] * 8 + k]
        ordered[:, k * CLUSTER : (k + 1) * CLUSTER] = upper[
            :, pl.ds(pl.multiple_of(block * CLUSTER, CLUSTER), CLUSTER)
        ]
    out[...] = multiply(halves(ordered[...]), (near[...], near_low[...]))


def less_far(place, value, got, got_pair, far, far_low, solved):
    panel = value.shape[1]
    solved[...] = value[...]

    @pl.when(place[1] != 0)
    def _():
        core = place[0]
        rows = [pl.ds(pl.multiple_of(c * panel, panel), panel) for c in (core, 1 - core)]
        total = value[...]
        for source, r in zip((got, got_pair), rows):
            total -= multiply(halves(source[...]), (far[r, :], far_low[r, :]))
        solved[...] = total


def pack(row, solved, out):
    out[...] = jnp.zeros(out.shape, out.dtype)
    left = lax.broadcasted_iota(jnp.int32, (32, 2 * ROWS), 1) < ROWS
    for g in range(4):
        low = solved[:32, g * 2 * ROWS : (g + 1) * 2 * ROWS]
        high = solved[32:, g * 2 * ROWS : (g + 1) * 2 * ROWS]
        out[8 * row + 2 * g] = jnp.where(left, low, pltpu.roll(high, ROWS, 1))
        out[8 * row + 2 * g + 1] = jnp.where(left, pltpu.roll(low, ROWS, 1), high)


def second_kernel(place, value, got, got_pair, far, far_low, solved, out):
    less_far(place, value, got, got_pair, far, far_low, solved)
    pack(place[6], solved, out)


def third_kernel(place, order, value, far, other, near, near_low, out, held, rows, ordered):
    part = value.shape[1] // 2
    collect(place, held, value, far, other)
    for a in range(4):
        for b in range(8):
            high, strip = a // 2, 8 * (a % 2) + b
            for q in range(2):
                start = 512 * q + 32 * strip + part * high
                rows[start : start + part, :] = held[a, b, part * q : part * (q + 1), :]
    for k in range(8):
        block = order[place[1] * 8 + k]
        taken = rows[pl.ds(pl.multiple_of((block % 8) * CLUSTER, CLUSTER), CLUSTER), :]
        ordered[k * CLUSTER : (k + 1) * CLUSTER, :] = jnp.where(
            block >= 8, pltpu.roll(taken, ROWS, 1), taken
        )
    first, second = halves(ordered[...])
    left = lax.broadcasted_iota(jnp.int32, ordered.shape, 1) < ROWS
    beside = pltpu.roll(second.astype(jnp.float32), ROWS, 1)
    beside = jnp.where(left, first.astype(jnp.float32), beside).astype(jnp.bfloat16)

    def one(u, v):
        return lax.dot_general(u, v, (((0,), (0,)), ((), ())), preferred_element_type=jnp.float32)

    both = one(beside, near[...])
    out[...] = both[:ROWS] + (both[ROWS:] + one(first, near_low[...])[:ROWS])


def last_kernel(place, scale, result, turned, out, rows):
    for b in range(8):
        block = turned[8 * place[6] + b]
        rows[64 * b : 64 * b + 32, :] = block
        rows[64 * b + 32 : 64 * b + 64, :] = pltpu.roll(block, ROWS, 1)
    both = (result[...] + rows[...].T[:ROWS]) * scale[0]
    out[...] = jnp.where(place[5] <= place[4], both, 0.0)


def kernel_call(kernel, scalars, out_shape, scratch, cost, *arrays, after=(), large=(), large_outs=0):
    arrays = (*arrays, *large)
    inputs = len(scalars) + len(arrays)

    def body(*refs):
        kernel(*refs[:inputs], *refs[inputs + len(after) :])

    vmem = pl.BlockSpec(memory_space=pltpu.VMEM)
    smem = pl.BlockSpec(memory_space=pltpu.SMEM)
    several = isinstance(out_shape, list)
    return pl.pallas_call(
        body,
        out_shape=out_shape,
        in_specs=[smem] * len(scalars)
        + [vmem] * (len(arrays) - len(large))
        + [pl.BlockSpec(memory_space=pl.ANY)] * (len(large) + len(after)),
        out_specs=[vmem] * (len(out_shape) - large_outs)
        + [pl.BlockSpec(memory_space=pl.ANY)] * large_outs
        if several
        else vmem,
        scratch_shapes=[pltpu.VMEM(shape, jnp.float32) for shape in scratch]
        + [pltpu.SemaphoreType.DMA((len(scratch),))] * bool(large),
        compiler_params=pltpu.CompilerParams(vmem_limit_bytes=40 << 20),
        cost_estimate=pl.CostEstimate(flops=int(cost * 1e9), bytes_accessed=int(cost * 3e6), transcendentals=0),
    )(*scalars, *arrays, *after)


def shape(*dims, dtype=jnp.float32):
    return jax.ShapeDtypeStruct(dims, dtype)


def sum_along(values, swapped):
    got = [
        lax.ppermute(values[step], ("pts", "lm"), plane_step(step, swapped)) for step in (1, 3, 2)
    ]
    return values[0] + got[0] + got[1] + got[2], got


def per_device(kernel_features, factor, diag_inverse, block_order):
    own = kernel_features
    points, panel = own.shape
    half, thin, part = points // 2, panel // 2, panel // 32
    i, j = lax.axis_index("pts"), lax.axis_index("lm")
    chip, core = j // 2, j % 2
    high, x, y = i // 16, (i // 4) % 4, i % 4
    first_core = core == 0
    group = i // 8
    row = jnp.where(group < j, 1, jnp.where(group > j, 0, j % 2))
    place = jnp.stack(
        [core, chip, jnp.where(first_core, x, y), jnp.where(first_core, y, x), j, group, row, x]
    ).astype(jnp.int32)
    order = block_order

    pair = lax.ppermute(own, "lm", OTHER_CORE)
    sent = lax.dynamic_slice_in_dim(own, (1 - chip) * half, half)
    across = [sent[:, at : at + w] for at, w in PIECES]
    pair, across[1] = lax.optimization_barrier((pair, across[1]))
    across = [lax.ppermute(value, "lm", OTHER_CHIP) for value in across]

    product = kernel_call(
        near_kernel, [place], shape(panel, panel + 2 * CLUSTER + thin), [], COSTS[0], own, pair
    )
    widths = [KEPT + thin + 2 * PIECES[0][1], 2 * PIECES[1][1]]
    early = kernel_call(
        early_kernel,
        [place],
        [shape(4, panel // 16, widths[0])] * 4,
        [(panel, 2 * PIECES[0][1])],
        COSTS[1],
        own,
        pair,
        across[0],
        product,
    )
    early_sum, arrived = sum_along(early, False)
    prepared = kernel_call(
        prepare_kernel,
        [place],
        [shape(2 * panel, half, dtype=jnp.bfloat16)] * 2,
        [],
        COSTS[3],
        own,
        pair,
        after=(early[0],),
    )
    across[1], *prepared_and = lax.optimization_barrier((across[1], *prepared, *arrived))
    prepared = prepared_and[:2]
    across[1] = lax.ppermute(across[1], "lm", OTHER_CORE)
    late = kernel_call(
        late_kernel,
        [place],
        [shape(4, panel // 16, widths[1])] * 4,
        [(panel, widths[1])],
        COSTS[3],
        *prepared,
        across[1],
        after=(early_sum,),
    )
    late_sum, _ = sum_along(late, False)
    parts = [jnp.concatenate([a, b], -1) for a, b in zip(early_sum, late_sum)]
    inverse = diag_inverse[0]
    near, near_low, far, far_low = kernel_call(
        inverse_kernel,
        [place],
        [shape(2 * panel, panel, dtype=jnp.bfloat16)] * 4,
        [(2 * panel, panel), (2 * panel, panel), (panel, panel)],
        COSTS[2],
        inverse,
        lax.ppermute(inverse, "lm", OTHER_CORE),
        large=(factor, lax.ppermute(factor[: 2 * panel], "lm", OTHER_CORE)),
        after=(early[0],),
    )
    parts, far_low = lax.optimization_barrier((parts, far_low))
    mine, _ = sum_along(parts, True)
    here, there = lax.optimization_barrier(
        tuple(lax.dynamic_slice_in_dim(mine, at * part, part) for at in (high, 1 - high))
    )
    far_here = lax.ppermute(here, "lm", OTHER_CHIP)
    far_there = lax.ppermute(there, ("pts", "lm"), other_high(2))
    here += lax.ppermute(there, ("pts", "lm"), other_high(0))
    away = far_here + far_there

    def spread(value, away):
        return value, away, lax.ppermute(jnp.stack([value, away]), "lm", OTHER_CORE)

    def hop(value):
        got = lax.ppermute(value, "lm", OTHER_CHIP)
        return value, got, lax.ppermute(got, "lm", OTHER_CORE), far, far_low

    def turned(packed):
        groups = turn_groups()
        return lax.all_to_all(packed, ("pts", "lm"), 0, 0, axis_index_groups=groups, tiled=True)

    square, packed = shape(ROWS, panel), shape(16, 32, 2 * ROWS)
    flops = 2
    width = here.shape[1]
    value = kernel_call(
        first_kernel,
        [place, order],
        square,
        [(4, part, width), (ROWS, 4 * panel), (ROWS, 2 * panel)],
        flops,
        *spread(here, away),
        near,
        near_low,
    )
    _, value = kernel_call(second_kernel, [place], [square, packed], [], flops, *hop(value))
    value = lax.dynamic_slice_in_dim(turned(value), 8 * row, 8)
    away = lax.ppermute(value, "lm", OTHER_CHIP)
    value = kernel_call(
        third_kernel,
        [place, order],
        square,
        [(4, 8, 32, 2 * ROWS), (2 * panel, 2 * ROWS), (2 * panel, 2 * ROWS)],
        flops,
        *spread(value, away),
        near,
        near_low,
    )
    result, value = kernel_call(second_kernel, [place], [square, packed], [], flops, *hop(value))
    scale = jnp.full((1,), 1.0 / (points * lax.axis_size("pts")), jnp.float32)
    return kernel_call(
        last_kernel, [place, scale], square, [(panel, 2 * ROWS)], 0, result, turned(value)
    )


def solution(mesh):
    placed = (P("pts", "lm"), P(None, "lm"), P("lm", None, None), P())
    return jax.shard_map(
        per_device, mesh=mesh, in_specs=placed, out_specs=P("pts", "lm"), check_vma=False
    )
```

```python
import jax
import jax.numpy as jnp
from jax import lax
from jax.experimental import pallas as pl
from jax.experimental.pallas import tpu as pltpu
from jax.sharding import PartitionSpec as P

PANEL = 512
CLUSTER = 128
COSTS = (40, 6, 4, 4)
PIECES = ((0, 128), (128, 384))
ROWS = 64
KEPT = 3 * CLUSTER

CELLS = [(zh, x, y) for zh in range(2) for x in range(4) for y in range(4)]


def pts_index(zh, x, y):
    return (zh * 4 + x) * 4 + y


def plane_step(step, swapped):
    pairs = []
    for z, x, y in CELLS:
        for j in range(4):
            if (j % 2 == 0) != swapped:
                to = pts_index(z, (x + step) % 4, y)
            else:
                to = pts_index(z, x, (y + step) % 4)
            pairs.append((pts_index(z, x, y) * 4 + j, to * 4 + j))
    return pairs


def other_high(k):
    return [
        (pts_index(z, x, y) * 4 + j, pts_index(1 - z, x, y) * 4 + (j ^ k))
        for z, x, y in CELLS
        for j in range(4)
    ]


OTHER_CHIP = [(k, k ^ 2) for k in range(4)]
OTHER_CORE = [(k, k ^ 1) for k in range(4)]


def turn_groups():
    rows = [((a, j), (j, a)) for a in range(4) for j in range(a + 1, 4)]
    rows += [((a, a), (a + 1, a + 1)) for a in (0, 2)]
    return [[(8 * a + b) * 4 + j for a, j in pair for b in range(8)] for pair in rows]


def halves(value):
    first = value.astype(jnp.bfloat16)
    return first, (value - first.astype(jnp.float32)).astype(jnp.bfloat16)


def contract(a, b):
    def one(u, v):
        return lax.dot_general(u, v, (((0,), (0,)), ((), ())), preferred_element_type=jnp.float32)

    return one(a[0], b[0]) + (one(a[0], b[1]) + one(a[1], b[0]))


def multiply(a, b):
    def one(u, v):
        return jnp.dot(u, v, preferred_element_type=jnp.float32)

    rows = a[0].shape[0]
    both = one(jnp.concatenate(a, 0), b[0])
    return both[:rows] + (both[rows:] + one(a[0], b[1]))


def write_strips(place, product, outs, own_product=None):
    core, first, second = place[0], place[2], place[3]
    start = 0
    if own_product is not None:
        block = lax.broadcasted_iota(jnp.int32, (32, KEPT), 1) // CLUSTER
        weight = jnp.where(block == 1, 1.0, 0.5)
        wrapped = PANEL + 2 * CLUSTER
        start = KEPT + own_product.shape[1] - wrapped
    for k in range(4):
        for m in range(4):
            f, g = (first + k) % 4, (second + m) % 4
            strip = jnp.where(core == 0, 4 * f + g, 4 * g + f)
            rows = pl.ds(pl.multiple_of(strip * 32, 32), 32)
            if own_product is not None:
                at = jnp.where(core == 0, f, g) * CLUSTER
                columns = pl.ds(pl.multiple_of(at, CLUSTER), KEPT)
                outs[k][m, :, :KEPT] = own_product[rows, columns] * weight
                outs[k][m, :, KEPT:start] = own_product[rows, wrapped:]
            outs[k][m, :, start:] = product[rows, :]


def near_kernel(place, own, pair, product):
    panel = own.shape[1]
    thin = panel // 2
    wrapped = panel + 2 * CLUSTER
    a = halves(own[...])
    square = contract(a, a)
    product[:, :panel] = square
    product[:, panel:wrapped] = square[:, : 2 * CLUSTER]

    @pl.when(place[0] == 0)
    def _():
        product[:, wrapped:] = contract(a, halves(pair[:, :thin]))

    @pl.when(place[0] != 0)
    def _():
        b = [part[:, thin:] for part in a]
        product[:, wrapped:] = contract(halves(pair[...]), b)


def early_kernel(place, own, pair, value, own_product, out0, out1, out2, out3, product):
    half, width = value.shape
    rows = pl.ds(pl.multiple_of(place[1] * half, half), half)
    b = halves(value[...])
    product[:, :width] = contract(b, halves(own[rows, :])).T
    product[:, width:] = contract(b, halves(pair[rows, :])).T
    write_strips(place, product, (out0, out1, out2, out3), own_product)


def prepare_kernel(place, own, pair, first, second):
    panel, half = own.shape[1], own.shape[0] // 2
    rows = pl.ds(pl.multiple_of(place[1] * half, half), half)
    for k, panel_of in enumerate((own, pair)):
        into = slice(k * panel, (k + 1) * panel)
        first[into, :], second[into, :] = halves(panel_of[rows, :].T)


def late_kernel(place, first, second, value, out0, out1, out2, out3, product):
    panel, width = first.shape[0] // 2, value.shape[1]
    b = halves(value[...])
    for k in range(2):
        rows = slice(k * panel, (k + 1) * panel)
        product[:, k * width : (k + 1) * width] = multiply((first[rows, :], second[rows, :]), b)
    write_strips(place, product, (out0, out1, out2, out3))


def inverse_kernel(
    place, inverse, pair_inverse, factor, pair_factor, near, near_low, far, far_low, above, pair_above, link, done
):
    panel = inverse.shape[0]
    start = pl.multiple_of(place[1] * 2 * panel, 2 * panel)
    copies = [
        pltpu.make_async_copy(factor.at[pl.ds(0, 2 * panel), :], above, done.at[0]),
        pltpu.make_async_copy(pair_factor.at[pl.ds(0, 2 * panel), :], pair_above, done.at[1]),
        pltpu.make_async_copy(factor.at[pl.ds(start, panel), :], link, done.at[2]),
    ]
    for copy in copies:
        copy.start()
    for copy in copies:
        copy.wait()
    d = halves(inverse[...])

    def put(high, low, rows, value):
        parts = halves(value)
        high[rows, :] = parts[0]
        low[rows, :] = parts[1]

    top, bottom = slice(0, panel), slice(panel, 2 * panel)

    @pl.when(place[0] == 0)
    def _():
        near[top, :], near_low[top, :] = d
        near[bottom, :] = jnp.zeros_like(d[0])
        near_low[bottom, :] = jnp.zeros_like(d[0])
        for rows in (top, bottom):
            put(far, far_low, rows, multiply(halves(above[rows, :]), d))

    @pl.when(place[0] != 0)
    def _():
        near[bottom, :], near_low[bottom, :] = d
        corner = -multiply(halves(pair_inverse[...]), halves(multiply(halves(link[...]), d)))
        put(near, near_low, top, corner)
        c = halves(corner)
        for rows in (top, bottom):
            value = multiply(halves(above[rows, :]), d) + multiply(halves(pair_above[rows, :]), c)
            put(far, far_low, rows, value)


def collect(place, held, value, far, other):
    j = place[4]
    held[j] = value[...]
    held[j ^ 2] = far[...]
    held[j ^ 1] = other[0]
    held[j ^ 3] = other[1]


def first_kernel(place, order, value, far, other, near, near_low, out, held, upper, ordered):
    part = value.shape[0]
    panel = near.shape[1]
    thin = panel // 2
    collect(place, held, value, far, other)

    def put(q, column, source, first, width):
        upper[part * q : part * (q + 1), column : column + width] = held[
            source, :, first : first + width
        ]

    nothing = jnp.zeros((part, CLUSTER), jnp.float32)
    for q in range(4):
        chip, core = divmod(q, 2)
        for t in range(4):
            start = q * panel + (place[7] + t) % 4 * CLUSTER
            columns = pl.ds(pl.multiple_of(start, CLUSTER), CLUSTER)
            kept = held[q, :, t * CLUSTER : (t + 1) * CLUSTER] if t < 3 else nothing
            upper[part * q : part * (q + 1), columns] = kept
        if core == 0:
            put(q, (q + 1) * panel, q, KEPT, thin)
            put(q, (q + 1) * panel + thin, q + 1, KEPT, thin)
        else:
            upper[part * q : part * (q + 1), (q - 1) * panel : q * panel] = jnp.zeros(
                (part, panel), jnp.float32
            )
        for c in range(2):
            first = KEPT + thin
            for (at, width), straight in zip(PIECES, (c == core, c != core)):
                column = (2 * (1 - chip) + c) * panel + at
                put(q, column, q if straight else q ^ 1, first + width * (not straight), width)
                first += 2 * width
    for k in range(8):
        block = order[place[1] * 8 + k]
        ordered[:, k * CLUSTER : (k + 1) * CLUSTER] = upper[
            :, pl.ds(pl.multiple_of(block * CLUSTER, CLUSTER), CLUSTER)
        ]
    out[...] = multiply(halves(ordered[...]), (near[...], near_low[...]))


def less_far(place, value, got, got_pair, far, far_low, solved):
    solved[...] = value[...]

    @pl.when(place[1] != 0)
    def _():
        first = place[0] == 0
        left = jnp.where(first, got[...], got_pair[...])
        right = jnp.where(first, got_pair[...], got[...])
        before = halves(jnp.concatenate([left, right], 1))
        solved[...] = value[...] - multiply(before, (far[...], far_low[...]))


def pack(row, solved, out):
    out[...] = jnp.zeros(out.shape, out.dtype)
    left = lax.broadcasted_iota(jnp.int32, (32, 2 * ROWS), 1) < ROWS
    for g in range(4):
        low = solved[:32, g * 2 * ROWS : (g + 1) * 2 * ROWS]
        high = solved[32:, g * 2 * ROWS : (g + 1) * 2 * ROWS]
        out[8 * row + 2 * g] = jnp.where(left, low, pltpu.roll(high, ROWS, 1))
        out[8 * row + 2 * g + 1] = jnp.where(left, pltpu.roll(low, ROWS, 1), high)


def second_kernel(place, value, got, got_pair, far, far_low, solved, out):
    less_far(place, value, got, got_pair, far, far_low, solved)
    pack(place[6], solved, out)


def third_kernel(place, order, value, far, other, near, near_low, out, held, rows, ordered):
    part = value.shape[1] // 2
    collect(place, held, value, far, other)
    for a in range(4):
        for b in range(8):
            high, strip = a // 2, 8 * (a % 2) + b
            for q in range(2):
                start = 512 * q + 32 * strip + part * high
                rows[start : start + part, :] = held[a, b, part * q : part * (q + 1), :]
    for k in range(8):
        block = order[place[1] * 8 + k]
        taken = rows[pl.ds(pl.multiple_of((block % 8) * CLUSTER, CLUSTER), CLUSTER), :]
        ordered[k * CLUSTER : (k + 1) * CLUSTER, :] = jnp.where(
            block >= 8, pltpu.roll(taken, ROWS, 1), taken
        )
    first, second = halves(ordered[...])
    left = lax.broadcasted_iota(jnp.int32, ordered.shape, 1) < ROWS
    beside = pltpu.roll(second.astype(jnp.float32), ROWS, 1)
    beside = jnp.where(left, first.astype(jnp.float32), beside).astype(jnp.bfloat16)

    def one(u, v):
        return lax.dot_general(u, v, (((0,), (0,)), ((), ())), preferred_element_type=jnp.float32)

    both = one(beside, near[...])
    out[...] = both[:ROWS] + (both[ROWS:] + one(first, near_low[...])[:ROWS])


def last_kernel(place, scale, result, turned, out, rows):
    for b in range(8):
        block = turned[8 * place[6] + b]
        rows[64 * b : 64 * b + 32, :] = block
        rows[64 * b + 32 : 64 * b + 64, :] = pltpu.roll(block, ROWS, 1)
    both = (result[...] + rows[...].T[:ROWS]) * scale[0]
    out[...] = jnp.where(place[5] <= place[4], both, 0.0)


def kernel_call(kernel, scalars, out_shape, scratch, cost, *arrays, after=(), large=(), large_outs=0):
    arrays = (*arrays, *large)
    inputs = len(scalars) + len(arrays)

    def body(*refs):
        kernel(*refs[:inputs], *refs[inputs + len(after) :])

    vmem = pl.BlockSpec(memory_space=pltpu.VMEM)
    smem = pl.BlockSpec(memory_space=pltpu.SMEM)
    several = isinstance(out_shape, list)
    return pl.pallas_call(
        body,
        out_shape=out_shape,
        in_specs=[smem] * len(scalars)
        + [vmem] * (len(arrays) - len(large))
        + [pl.BlockSpec(memory_space=pl.ANY)] * (len(large) + len(after)),
        out_specs=[vmem] * (len(out_shape) - large_outs)
        + [pl.BlockSpec(memory_space=pl.ANY)] * large_outs
        if several
        else vmem,
        scratch_shapes=[pltpu.VMEM(shape, jnp.float32) for shape in scratch]
        + [pltpu.SemaphoreType.DMA((len(scratch),))] * bool(large),
        compiler_params=pltpu.CompilerParams(vmem_limit_bytes=40 << 20),
        cost_estimate=pl.CostEstimate(flops=int(cost * 1e9), bytes_accessed=int(cost * 3e6), transcendentals=0),
    )(*scalars, *arrays, *after)


def shape(*dims, dtype=jnp.float32):
    return jax.ShapeDtypeStruct(dims, dtype)


def sum_along(values, swapped):
    got = [
        lax.ppermute(values[step], ("pts", "lm"), plane_step(step, swapped)) for step in (1, 3, 2)
    ]
    return values[0] + got[0] + got[1] + got[2], got


def per_device(kernel_features, factor, diag_inverse, block_order):
    own = kernel_features
    points, panel = own.shape
    half, thin, part = points // 2, panel // 2, panel // 32
    i, j = lax.axis_index("pts"), lax.axis_index("lm")
    chip, core = j // 2, j % 2
    high, x, y = i // 16, (i // 4) % 4, i % 4
    first_core = core == 0
    group = i // 8
    row = jnp.where(group < j, 1, jnp.where(group > j, 0, j % 2))
    place = jnp.stack(
        [core, chip, jnp.where(first_core, x, y), jnp.where(first_core, y, x), j, group, row, x]
    ).astype(jnp.int32)
    order = block_order

    pair = lax.ppermute(own, "lm", OTHER_CORE)
    sent = lax.dynamic_slice_in_dim(own, (1 - chip) * half, half)
    across = [sent[:, at : at + w] for at, w in PIECES]
    pair, across[1] = lax.optimization_barrier((pair, across[1]))
    across = [lax.ppermute(value, "lm", OTHER_CHIP) for value in across]

    product = kernel_call(
        near_kernel, [place], shape(panel, panel + 2 * CLUSTER + thin), [], COSTS[0], own, pair
    )
    widths = [KEPT + thin + 2 * PIECES[0][1], 2 * PIECES[1][1]]
    early = kernel_call(
        early_kernel,
        [place],
        [shape(4, panel // 16, widths[0])] * 4,
        [(panel, 2 * PIECES[0][1])],
        COSTS[1],
        own,
        pair,
        across[0],
        product,
    )
    early_sum, arrived = sum_along(early, False)
    prepared = kernel_call(
        prepare_kernel,
        [place],
        [shape(2 * panel, half, dtype=jnp.bfloat16)] * 2,
        [],
        COSTS[3],
        own,
        pair,
        after=(early[0],),
    )
    across[1], *prepared_and = lax.optimization_barrier((across[1], *prepared, *arrived))
    prepared = prepared_and[:2]
    across[1] = lax.ppermute(across[1], "lm", OTHER_CORE)
    late = kernel_call(
        late_kernel,
        [place],
        [shape(4, panel // 16, widths[1])] * 4,
        [(panel, widths[1])],
        COSTS[3],
        *prepared,
        across[1],
        after=(early_sum,),
    )
    late_sum, _ = sum_along(late, False)
    parts = [jnp.concatenate([a, b], -1) for a, b in zip(early_sum, late_sum)]
    inverse = diag_inverse[0]
    near, near_low, far, far_low = kernel_call(
        inverse_kernel,
        [place],
        [shape(2 * panel, panel, dtype=jnp.bfloat16)] * 4,
        [(2 * panel, panel), (2 * panel, panel), (panel, panel)],
        COSTS[2],
        inverse,
        lax.ppermute(inverse, "lm", OTHER_CORE),
        large=(factor, lax.ppermute(factor[: 2 * panel], "lm", OTHER_CORE)),
        after=(early[0],),
    )
    parts, far_low = lax.optimization_barrier((parts, far_low))
    mine, _ = sum_along(parts, True)
    here, there = lax.optimization_barrier(
        tuple(lax.dynamic_slice_in_dim(mine, at * part, part) for at in (high, 1 - high))
    )
    far_here = lax.ppermute(here, "lm", OTHER_CHIP)
    far_there = lax.ppermute(there, ("pts", "lm"), other_high(2))
    here += lax.ppermute(there, ("pts", "lm"), other_high(0))
    away = far_here + far_there

    def spread(value, away):
        return value, away, lax.ppermute(jnp.stack([value, away]), "lm", OTHER_CORE)

    def hop(value):
        got = lax.ppermute(value, "lm", OTHER_CHIP)
        return value, got, lax.ppermute(got, "lm", OTHER_CORE), far, far_low

    def turned(packed):
        groups = turn_groups()
        return lax.all_to_all(packed, ("pts", "lm"), 0, 0, axis_index_groups=groups, tiled=True)

    square, packed = shape(ROWS, panel), shape(16, 32, 2 * ROWS)
    flops = 2
    width = here.shape[1]
    value = kernel_call(
        first_kernel,
        [place, order],
        square,
        [(4, part, width), (ROWS, 4 * panel), (ROWS, 2 * panel)],
        flops,
        *spread(here, away),
        near,
        near_low,
    )
    _, value = kernel_call(second_kernel, [place], [square, packed], [], flops, *hop(value))
    value = lax.dynamic_slice_in_dim(turned(value), 8 * row, 8)
    away = lax.ppermute(value, "lm", OTHER_CHIP)
    value = kernel_call(
        third_kernel,
        [place, order],
        square,
        [(4, 8, 32, 2 * ROWS), (2 * panel, 2 * ROWS), (2 * panel, 2 * ROWS)],
        flops,
        *spread(value, away),
        near,
        near_low,
    )
    result, value = kernel_call(second_kernel, [place], [square, packed], [], flops, *hop(value))
    scale = jnp.full((1,), 1.0 / (points * lax.axis_size("pts")), jnp.float32)
    return kernel_call(
        last_kernel, [place, scale], square, [(panel, 2 * ROWS)], 0, result, turned(value)
    )


def solution(mesh):
    placed = (P("pts", "lm"), P(None, "lm"), P("lm", None, None), P())
    return jax.shard_map(
        per_device, mesh=mesh, in_specs=placed, out_specs=P("pts", "lm"), check_vma=False
    )
```

```python
import jax
import jax.numpy as jnp
from jax import lax
from jax.experimental import pallas as pl
from jax.experimental.pallas import tpu as pltpu
from jax.sharding import PartitionSpec as P

PANEL = 512
CLUSTER = 128
COSTS = (40, 6, 4, 4)
PIECES = ((0, 128), (128, 384))
ROWS = 64
KEPT = 3 * CLUSTER

CELLS = [(zh, x, y) for zh in range(2) for x in range(4) for y in range(4)]


def pts_index(zh, x, y):
    return (zh * 4 + x) * 4 + y


def plane_step(step, swapped):
    pairs = []
    for z, x, y in CELLS:
        for j in range(4):
            if (j % 2 == 0) != swapped:
                to = pts_index(z, (x + step) % 4, y)
            else:
                to = pts_index(z, x, (y + step) % 4)
            pairs.append((pts_index(z, x, y) * 4 + j, to * 4 + j))
    return pairs


def other_high(k):
    return [
        (pts_index(z, x, y) * 4 + j, pts_index(1 - z, x, y) * 4 + (j ^ k))
        for z, x, y in CELLS
        for j in range(4)
    ]


OTHER_CHIP = [(k, k ^ 2) for k in range(4)]
OTHER_CORE = [(k, k ^ 1) for k in range(4)]


def turn_groups():
    rows = [((a, j), (j, a)) for a in range(4) for j in range(a + 1, 4)]
    rows += [((a, a), (a + 1, a + 1)) for a in (0, 2)]
    return [[(8 * a + b) * 4 + j for a, j in pair for b in range(8)] for pair in rows]


def halves(value):
    first = value.astype(jnp.bfloat16)
    return first, (value - first.astype(jnp.float32)).astype(jnp.bfloat16)


def contract(a, b):
    def one(u, v):
        return lax.dot_general(u, v, (((0,), (0,)), ((), ())), preferred_element_type=jnp.float32)

    return one(a[0], b[0]) + (one(a[0], b[1]) + one(a[1], b[0]))


def multiply(a, b):
    def one(u, v):
        return jnp.dot(u, v, preferred_element_type=jnp.float32)

    rows = a[0].shape[0]
    both = one(jnp.concatenate(a, 0), b[0])
    return both[:rows] + (both[rows:] + one(a[0], b[1]))


def write_strips(place, product, outs, own_product=None):
    core, first, second = place[0], place[2], place[3]
    start = 0
    if own_product is not None:
        block = lax.broadcasted_iota(jnp.int32, (32, KEPT), 1) // CLUSTER
        weight = jnp.where(block == 1, 1.0, 0.5)
        wrapped = PANEL + 2 * CLUSTER
        start = KEPT + own_product.shape[1] - wrapped
    for k in range(4):
        for m in range(4):
            f, g = (first + k) % 4, (second + m) % 4
            strip = jnp.where(core == 0, 4 * f + g, 4 * g + f)
            rows = pl.ds(pl.multiple_of(strip * 32, 32), 32)
            if own_product is not None:
                at = jnp.where(core == 0, f, g) * CLUSTER
                columns = pl.ds(pl.multiple_of(at, CLUSTER), KEPT)
                outs[k][m, :, :KEPT] = own_product[rows, columns] * weight
                outs[k][m, :, KEPT:start] = own_product[rows, wrapped:]
            outs[k][m, :, start:] = product[rows, :]


def near_kernel(place, own, pair, product):
    panel = own.shape[1]
    thin = panel // 2
    wrapped = panel + 2 * CLUSTER
    a = halves(own[...])
    square = contract(a, a)
    product[:, :panel] = square
    product[:, panel:wrapped] = square[:, : 2 * CLUSTER]

    @pl.when(place[0] == 0)
    def _():
        product[:, wrapped:] = contract(a, halves(pair[:, :thin]))

    @pl.when(place[0] != 0)
    def _():
        b = [part[:, thin:] for part in a]
        product[:, wrapped:] = contract(halves(pair[...]), b)


def early_kernel(place, own, pair, value, own_product, out0, out1, out2, out3, product):
    half, width = value.shape
    rows = pl.ds(pl.multiple_of(place[1] * half, half), half)
    b = halves(value[...])
    product[:, :width] = contract(b, halves(own[rows, :])).T
    product[:, width:] = contract(b, halves(pair[rows, :])).T
    write_strips(place, product, (out0, out1, out2, out3), own_product)


def prepare_kernel(place, own, pair, first, second):
    panel, half = own.shape[1], own.shape[0] // 2
    rows = pl.ds(pl.multiple_of(place[1] * half, half), half)
    for k, panel_of in enumerate((own, pair)):
        into = slice(k * panel, (k + 1) * panel)
        first[into, :], second[into, :] = halves(panel_of[rows, :].T)


def late_kernel(place, first, second, value, out0, out1, out2, out3, product):
    panel, width = first.shape[0] // 2, value.shape[1]
    b = halves(value[...])
    for k in range(2):
        rows = slice(k * panel, (k + 1) * panel)
        product[:, k * width : (k + 1) * width] = multiply((first[rows, :], second[rows, :]), b)
    write_strips(place, product, (out0, out1, out2, out3))


def inverse_kernel(
    place, inverse, pair_inverse, factor, pair_factor, near, near_low, far, far_low, above, pair_above, link, done
):
    panel = inverse.shape[0]
    start = pl.multiple_of(place[1] * 2 * panel, 2 * panel)
    copies = [
        pltpu.make_async_copy(factor.at[pl.ds(0, 2 * panel), :], above, done.at[0]),
        pltpu.make_async_copy(pair_factor.at[pl.ds(0, 2 * panel), :], pair_above, done.at[1]),
        pltpu.make_async_copy(factor.at[pl.ds(start, panel), :], link, done.at[2]),
    ]
    for copy in copies:
        copy.start()
    for copy in copies:
        copy.wait()
    d = halves(inverse[...])

    def put(high, low, rows, value):
        parts = halves(value)
        high[rows, :] = parts[0]
        low[rows, :] = parts[1]

    top, bottom = slice(0, panel), slice(panel, 2 * panel)

    @pl.when(place[0] == 0)
    def _():
        near[top, :], near_low[top, :] = d
        near[bottom, :] = jnp.zeros_like(d[0])
        near_low[bottom, :] = jnp.zeros_like(d[0])
        for rows in (top, bottom):
            put(far, far_low, rows, multiply(halves(above[rows, :]), d))

    @pl.when(place[0] != 0)
    def _():
        near[bottom, :], near_low[bottom, :] = d
        corner = -multiply(halves(pair_inverse[...]), halves(multiply(halves(link[...]), d)))
        put(near, near_low, top, corner)
        c = halves(corner)
        for rows in (top, bottom):
            value = multiply(halves(above[rows, :]), d) + multiply(halves(pair_above[rows, :]), c)
            put(far, far_low, rows, value)


def collect(place, held, value, far, other):
    j = place[4]
    held[j] = value[...]
    held[j ^ 2] = far[...]
    held[j ^ 1] = other[0]
    held[j ^ 3] = other[1]


def first_kernel(place, order, value, far, other, near, near_low, out, held, upper, ordered):
    part = value.shape[0]
    panel = near.shape[1]
    thin = panel // 2
    collect(place, held, value, far, other)

    def put(q, column, source, first, width):
        upper[part * q : part * (q + 1), column : column + width] = held[
            source, :, first : first + width
        ]

    nothing = jnp.zeros((part, CLUSTER), jnp.float32)
    for q in range(4):
        chip, core = divmod(q, 2)
        for t in range(4):
            start = q * panel + (place[7] + t) % 4 * CLUSTER
            columns = pl.ds(pl.multiple_of(start, CLUSTER), CLUSTER)
            kept = held[q, :, t * CLUSTER : (t + 1) * CLUSTER] if t < 3 else nothing
            upper[part * q : part * (q + 1), columns] = kept
        if core == 0:
            put(q, (q + 1) * panel, q, KEPT, thin)
            put(q, (q + 1) * panel + thin, q + 1, KEPT, thin)
        else:
            upper[part * q : part * (q + 1), (q - 1) * panel : q * panel] = jnp.zeros(
                (part, panel), jnp.float32
            )
        for c in range(2):
            first = KEPT + thin
            for (at, width), straight in zip(PIECES, (c == core, c != core)):
                column = (2 * (1 - chip) + c) * panel + at
                put(q, column, q if straight else q ^ 1, first + width * (not straight), width)
                first += 2 * width
    for k in range(8):
        block = order[place[1] * 8 + k]
        ordered[:, k * CLUSTER : (k + 1) * CLUSTER] = upper[
            :, pl.ds(pl.multiple_of(block * CLUSTER, CLUSTER), CLUSTER)
        ]
    out[...] = multiply(halves(ordered[...]), (near[...], near_low[...]))


def less_far(place, value, got, got_pair, far, far_low, solved):
    solved[...] = value[...]

    @pl.when(place[1] != 0)
    def _():
        first = place[0] == 0
        left = jnp.where(first, got[...], got_pair[...])
        right = jnp.where(first, got_pair[...], got[...])
        before = halves(jnp.concatenate([left, right], 1))
        solved[...] = value[...] - multiply(before, (far[...], far_low[...]))


def pack(row, solved, out):
    out[...] = jnp.zeros(out.shape, out.dtype)
    left = lax.broadcasted_iota(jnp.int32, (32, 2 * ROWS), 1) < ROWS
    for g in range(4):
        low = solved[:32, g * 2 * ROWS : (g + 1) * 2 * ROWS]
        high = solved[32:, g * 2 * ROWS : (g + 1) * 2 * ROWS]
        out[8 * row + 2 * g] = jnp.where(left, low, pltpu.roll(high, ROWS, 1))
        out[8 * row + 2 * g + 1] = jnp.where(left, pltpu.roll(low, ROWS, 1), high)


def second_kernel(place, value, got, got_pair, far, far_low, solved, out):
    less_far(place, value, got, got_pair, far, far_low, solved)
    pack(place[6], solved, out)


def third_kernel(place, order, value, far, other, near, near_low, out, held, rows, ordered):
    part = value.shape[1] // 2
    collect(place, held, value, far, other)
    for a in range(4):
        for b in range(8):
            high, strip = a // 2, 8 * (a % 2) + b
            for q in range(2):
                start = 512 * q + 32 * strip + part * high
                rows[start : start + part, :] = held[a, b, part * q : part * (q + 1), :]
    for k in range(8):
        block = order[place[1] * 8 + k]
        taken = rows[pl.ds(pl.multiple_of((block % 8) * CLUSTER, CLUSTER), CLUSTER), :]
        ordered[k * CLUSTER : (k + 1) * CLUSTER, :] = jnp.where(
            block >= 8, pltpu.roll(taken, ROWS, 1), taken
        )
    first, second = halves(ordered[...])
    left = lax.broadcasted_iota(jnp.int32, ordered.shape, 1) < ROWS
    beside = pltpu.roll(second.astype(jnp.float32), ROWS, 1)
    beside = jnp.where(left, first.astype(jnp.float32), beside).astype(jnp.bfloat16)

    def one(u, v):
        return lax.dot_general(u, v, (((0,), (0,)), ((), ())), preferred_element_type=jnp.float32)

    both = one(beside, near[...])
    out[...] = both[:ROWS] + (both[ROWS:] + one(first, near_low[...])[:ROWS])


def last_kernel(place, scale, result, turned, out, rows):
    for b in range(8):
        block = turned[8 * place[6] + b]
        rows[64 * b : 64 * b + 32, :] = block
        rows[64 * b + 32 : 64 * b + 64, :] = pltpu.roll(block, ROWS, 1)
    both = (result[...] + rows[...].T[:ROWS]) * scale[0]
    out[...] = jnp.where(place[5] <= place[4], both, 0.0)


def kernel_call(kernel, scalars, out_shape, scratch, cost, *arrays, after=(), large=(), large_outs=0):
    arrays = (*arrays, *large)
    inputs = len(scalars) + len(arrays)

    def body(*refs):
        kernel(*refs[:inputs], *refs[inputs + len(after) :])

    vmem = pl.BlockSpec(memory_space=pltpu.VMEM)
    smem = pl.BlockSpec(memory_space=pltpu.SMEM)
    several = isinstance(out_shape, list)
    return pl.pallas_call(
        body,
        out_shape=out_shape,
        in_specs=[smem] * len(scalars)
        + [vmem] * (len(arrays) - len(large))
        + [pl.BlockSpec(memory_space=pl.ANY)] * (len(large) + len(after)),
        out_specs=[vmem] * (len(out_shape) - large_outs)
        + [pl.BlockSpec(memory_space=pl.ANY)] * large_outs
        if several
        else vmem,
        scratch_shapes=[pltpu.VMEM(shape, jnp.float32) for shape in scratch]
        + [pltpu.SemaphoreType.DMA((len(scratch),))] * bool(large),
        compiler_params=pltpu.CompilerParams(vmem_limit_bytes=40 << 20),
        cost_estimate=pl.CostEstimate(flops=int(cost * 1e9), bytes_accessed=int(cost * 3e6), transcendentals=0),
    )(*scalars, *arrays, *after)


def shape(*dims, dtype=jnp.float32):
    return jax.ShapeDtypeStruct(dims, dtype)


def sum_along(values, swapped):
    got = [
        lax.ppermute(values[step], ("pts", "lm"), plane_step(step, swapped)) for step in (1, 3, 2)
    ]
    return values[0] + got[0] + got[1] + got[2], got


def per_device(kernel_features, factor, diag_inverse, block_order):
    own = kernel_features
    points, panel = own.shape
    half, thin, part = points // 2, panel // 2, panel // 32
    i, j = lax.axis_index("pts"), lax.axis_index("lm")
    chip, core = j // 2, j % 2
    high, x, y = i // 16, (i // 4) % 4, i % 4
    first_core = core == 0
    group = i // 8
    row = jnp.where(group < j, 1, jnp.where(group > j, 0, j % 2))
    place = jnp.stack(
        [core, chip, jnp.where(first_core, x, y), jnp.where(first_core, y, x), j, group, row, x]
    ).astype(jnp.int32)
    order = block_order

    pair = lax.ppermute(own, "lm", OTHER_CORE)
    sent = lax.dynamic_slice_in_dim(own, (1 - chip) * half, half)
    across = [sent[:, at : at + w] for at, w in PIECES]
    pair, across[1] = lax.optimization_barrier((pair, across[1]))
    across = [lax.ppermute(value, "lm", OTHER_CHIP) for value in across]

    product = kernel_call(
        near_kernel, [place], shape(panel, panel + 2 * CLUSTER + thin), [], COSTS[0], own, pair
    )
    widths = [KEPT + thin + 2 * PIECES[0][1], 2 * PIECES[1][1]]
    early = kernel_call(
        early_kernel,
        [place],
        [shape(4, panel // 16, widths[0])] * 4,
        [(panel, 2 * PIECES[0][1])],
        COSTS[1],
        own,
        pair,
        across[0],
        product,
    )
    early_sum, arrived = sum_along(early, False)
    prepared = kernel_call(
        prepare_kernel,
        [place],
        [shape(2 * panel, half, dtype=jnp.bfloat16)] * 2,
        [],
        COSTS[3],
        own,
        pair,
        after=(early[0],),
    )
    across[1], *prepared_and = lax.optimization_barrier((across[1], *prepared, *arrived))
    prepared = prepared_and[:2]
    across[1] = lax.ppermute(across[1], "lm", OTHER_CORE)
    late = kernel_call(
        late_kernel,
        [place],
        [shape(4, panel // 16, widths[1])] * 4,
        [(panel, widths[1])],
        COSTS[3],
        *prepared,
        across[1],
        after=tuple(arrived),
    )
    late_sum, _ = sum_along(late, False)
    parts = [jnp.concatenate([a, b], -1) for a, b in zip(early_sum, late_sum)]
    inverse = diag_inverse[0]
    near, near_low, far, far_low = kernel_call(
        inverse_kernel,
        [place],
        [shape(2 * panel, panel, dtype=jnp.bfloat16)] * 4,
        [(2 * panel, panel), (2 * panel, panel), (panel, panel)],
        COSTS[2],
        inverse,
        lax.ppermute(inverse, "lm", OTHER_CORE),
        large=(factor, lax.ppermute(factor[: 2 * panel], "lm", OTHER_CORE)),
        after=(early[0],),
    )
    parts, far_low = lax.optimization_barrier((parts, far_low))
    mine, _ = sum_along(parts, True)
    here, there = lax.optimization_barrier(
        tuple(lax.dynamic_slice_in_dim(mine, at * part, part) for at in (high, 1 - high))
    )
    far_here = lax.ppermute(here, "lm", OTHER_CHIP)
    far_there = lax.ppermute(there, ("pts", "lm"), other_high(2))
    here += lax.ppermute(there, ("pts", "lm"), other_high(0))
    away = far_here + far_there

    def spread(value, away):
        return value, away, lax.ppermute(jnp.stack([value, away]), "lm", OTHER_CORE)

    def hop(value):
        got = lax.ppermute(value, "lm", OTHER_CHIP)
        return value, got, lax.ppermute(got, "lm", OTHER_CORE), far, far_low

    def turned(packed):
        groups = turn_groups()
        return lax.all_to_all(packed, ("pts", "lm"), 0, 0, axis_index_groups=groups, tiled=True)

    square, packed = shape(ROWS, panel), shape(16, 32, 2 * ROWS)
    flops = 2
    width = here.shape[1]
    value = kernel_call(
        first_kernel,
        [place, order],
        square,
        [(4, part, width), (ROWS, 4 * panel), (ROWS, 2 * panel)],
        flops,
        *spread(here, away),
        near,
        near_low,
    )
    _, value = kernel_call(second_kernel, [place], [square, packed], [], flops, *hop(value))
    value = lax.dynamic_slice_in_dim(turned(value), 8 * row, 8)
    away = lax.ppermute(value, "lm", OTHER_CHIP)
    value = kernel_call(
        third_kernel,
        [place, order],
        square,
        [(4, 8, 32, 2 * ROWS), (2 * panel, 2 * ROWS), (2 * panel, 2 * ROWS)],
        flops,
        *spread(value, away),
        near,
        near_low,
    )
    result, value = kernel_call(second_kernel, [place], [square, packed], [], flops, *hop(value))
    scale = jnp.full((1,), 1.0 / (points * lax.axis_size("pts")), jnp.float32)
    return kernel_call(
        last_kernel, [place, scale], square, [(panel, 2 * ROWS)], 0, result, turned(value)
    )


def solution(mesh):
    placed = (P("pts", "lm"), P(None, "lm"), P("lm", None, None), P())
    return jax.shard_map(
        per_device, mesh=mesh, in_specs=placed, out_specs=P("pts", "lm"), check_vma=False
    )
```
